1024 devices in a mesh: comp: 16 (over x, z_hi), tile: 64 (over z_lo, y, core).
Axes of the slice: x: 4, y: 8, z: 16 (z_hi: 4, z_lo: 4; z = z_hi * 4 + z_lo), core: 2. Of those that a mesh axis runs over, the one named last changes fastest.
Arguments:
- atmos_state: float32 [128, 1024, 128], P('comp', 'tile'), may hold values from -6 to 6
- wind_field: bfloat16 [2, 128, 1024, 128], P(None, 'comp', 'tile'), may hold values from -5 to 5
- ocean_height: float32 [512, 8192], P('comp', 'tile'), may hold values from -6 to 6
- ocean_potential: float32 [512, 8192], P('comp', 'tile'), may hold values from -6 to 6
- ocean_neighbors: int32 [6, 512, 8192], P(None, 'comp', 'tile'), may hold values from 0 to 4419, as said below
- ocean_coupling: float32 [6, 512, 8192], P(None, 'comp', 'tile'), may hold values from 0.1 to 0.5
- downward_source: int32 [16, 4096, 128], P('comp', 'tile'), may hold values from 0 to 127, as said below
- downward_target: int32 [16, 4096, 128], P('comp', 'tile'), may hold values from 0 to 4095, as said below
- downward_weight: float32 [16, 4096, 128], P('comp', 'tile'), may hold values from 0.3 to 1.2
- upward_source: int32 [16, 4096, 128], P('comp', 'tile'), may hold values from 0 to 4095, as said below
- upward_target: int32 [16, 4096, 128], P('comp', 'tile'), may hold values from 0 to 127, as said below
- upward_weight: float32 [16, 4096, 128], P('comp', 'tile'), may hold values from 0.05 to 0.3
Outputs:
- atmos_out: float32 [128, 1024, 128], P('comp', 'tile')
- height_out: float32 [512, 8192], P('comp', 'tile')
- potential_out: float32 [512, 8192], P('comp', 'tile')
- surface_flux: float32 [128, 1024], P('comp', 'tile')
The draws below stay inside these ranges and needn't reach their ends.
Inputs may be any that keep to these rules, and one draw needn't show every extreme that they name: `ocean_neighbors`: the six entries of a cell are distinct and name the four cells beside it along the two dimensions and one of the two diagonal pairs. `downward_source`: within a row of devices the ocean's blocks are laid out differently from the atmosphere's, so the surface under one ocean block is spread over all devices of the row; band p of a device's local points (flat order, p * 8 * 16 // 64 onward, 2 of them) lies over row-peer p. Entries for peer p name points of band p. `downward_target`: entries from peer p name ocean cells of band p of the receiving device's cells (flat order, 64 of them from p * 32 * 2). `upward_source`: entries for peer p name ocean cells of band p of the sending device's cells (flat order, 64 of them from p * 32 * 2). `upward_target`: entries from peer p name surface points of band p of the receiving device's points (flat order, 2 of them from p * 8 * 16 // 64).
All inputs are finite; a program needn't handle non-finite values.
Results may differ from the reference program's by a relative error of at most 0.0003.
Values sent between devices are 32-bit elements; how exact they have to be, the bound alone decides.
A program may use at most 32 MiB of HBM per device.

```python
import jax
import jax.numpy as jnp
import numpy as np
from jax import lax

NP = 4
LEV = 128
OX = 32
OY = 128
SUBSTEPS = 2
SUBCYCLES = 8
AX = 8
AY = 16
NXA = 128
NYA = 1024
OXT = 512
OYT = 8192
SLOT = 128
N_COMP = 16
N_TILE = 64


def draw_ocean_neighbors(key, part):
    choose = jax.random.randint(jax.random.fold_in(key, 17), (OXT, OYT), 0, 2)
    row_local = jnp.arange(OXT, dtype=jnp.int32)[:, None] % OX
    col_local = jnp.arange(OYT, dtype=jnp.int32)[None, :] % OY
    corner = (row_local == 0) & (col_local == 0) | (row_local == OX - 1) & (col_local == OY - 1)
    choose = jnp.where(corner, 0, choose)
    diagonal = 1 - 2 * choose
    zeros_grid = jnp.zeros((OXT, OYT), jnp.int32)
    offset_row = jnp.stack([zeros_grid - 1, zeros_grid + 1, zeros_grid, zeros_grid, zeros_grid + 1, zeros_grid - 1])
    offset_col = jnp.stack([zeros_grid, zeros_grid, zeros_grid - 1, zeros_grid + 1, diagonal, 0 - diagonal])
    flat_index = (row_local[None] + 1 + offset_row) * (OY + 2) + (col_local[None] + 1 + offset_col)
    return flat_index.astype(jnp.int32)


def banded_table(key, extent):
    band = extent // N_TILE
    peer = (jnp.arange(N_TILE * N_TILE, dtype=jnp.int32) % N_TILE)[None, :, None]
    within = jax.random.randint(key, (N_COMP, N_TILE * N_TILE, SLOT), 0, band)
    return (peer * band + within).astype(jnp.int32)


def draw_downward_source(key, part):
    return banded_table(jax.random.fold_in(key, 31), AX * AY)


def draw_downward_target(key, part):
    return banded_table(jax.random.fold_in(key, 37), OX * OY)


def draw_upward_source(key, part):
    return banded_table(jax.random.fold_in(key, 41), OX * OY)


def draw_upward_target(key, part):
    return banded_table(jax.random.fold_in(key, 43), AX * AY)


def block_levels(rng, shape, cuts, low, high):
    level = 1.0
    for axis_at, parts in cuts:
        steps = jax.random.uniform(jax.random.fold_in(jax.random.fold_in(rng, 6), axis_at), (parts,), jnp.float32, low / len(cuts), high / len(cuts))
        level = level * jnp.repeat(jnp.exp(steps), shape[axis_at] // parts).reshape((-1,) + (1,) * (len(shape) - 1 - axis_at))
    return level


def scatter_about(own_key, shape, width, limit, split=(), kind=jnp.bfloat16):
    values = jax.random.normal(own_key, shape, jnp.float32) * width
    if len(split) > 0:
        values = block_levels(own_key, shape, split, -0.22, 0.18) * values
    return jnp.clip(values, min=-limit, max=limit).astype(kind)


def setup_inputs(seed: int = 0) -> dict:
    keys = jax.random.split(jax.random.key(seed), 13)
    return {
        "atmos_state": scatter_about(keys[0], (NXA, NYA, LEV), 1.0, 6.0, ((0, 16), (1, 64)), jnp.float32),
        "wind_field": scatter_about(keys[1], (2, NXA, NYA, LEV), 1.0, 5.0, ((1, 16), (2, 64))),
        "ocean_height": scatter_about(keys[2], (OXT, OYT), 1.0, 6.0, ((0, 16), (1, 64)), jnp.float32),
        "ocean_potential": scatter_about(keys[3], (OXT, OYT), 1.0, 6.0, ((0, 16), (1, 64)), jnp.float32),
        "ocean_neighbors": draw_ocean_neighbors(jax.random.fold_in(keys[12], 71), 0),
        "ocean_coupling": jnp.clip(0.1 + 0.4 * jax.random.uniform(keys[5], (6, OXT, OYT), jnp.float32) ** block_levels(keys[5], (6, OXT, OYT), ((1, 16), (2, 64)), -0.2, 0.2), 0.1, 0.5),
        "downward_source": draw_downward_source(jax.random.fold_in(keys[12], 71), 0),
        "downward_target": draw_downward_target(jax.random.fold_in(keys[12], 71), 0),
        "downward_weight": jnp.clip(0.3 + 0.90000004 * jax.random.uniform(keys[8], (N_COMP, N_TILE * N_TILE, SLOT), jnp.float32) ** block_levels(keys[8], (N_COMP, N_TILE * N_TILE, SLOT), ((0, 16), (1, 64)), -0.2, 0.2), 0.3, 1.2),
        "upward_source": draw_upward_source(jax.random.fold_in(keys[12], 71), 0),
        "upward_target": draw_upward_target(jax.random.fold_in(keys[12], 71), 0),
        "upward_weight": jnp.clip(0.05 + 0.25 * jax.random.uniform(keys[11], (N_COMP, N_TILE * N_TILE, SLOT), jnp.float32) ** block_levels(keys[11], (N_COMP, N_TILE * N_TILE, SLOT), ((0, 16), (1, 64)), -0.2, 0.2), 0.05, 0.3),
    }


atmos_step = 0.05
viscosity = 0.05
ocean_step = 0.2
wave_speed = 1.0
friction = 0.05

def gll_derivative():
    points = np.array([-1.0, -1.0 / np.sqrt(5.0), 1.0 / np.sqrt(5.0), 1.0])
    weights = np.array([1.0 / np.prod([points[j] - points[k] for k in range(4) if k != j]) for j in range(4)])
    matrix = np.zeros((4, 4))
    for i in range(4):
        for j in range(4):
            if i != j:
                matrix[i, j] = weights[j] / weights[i] / (points[i] - points[j])
        matrix[i, i] = -np.sum(matrix[i])
    return matrix

def along_first(values, matrix):
    extent_rows, extent_cols, levels = values.shape
    shaped = values.reshape(extent_rows // NP, NP, extent_cols, levels)
    result = jnp.einsum('ik,ekyl->eiyl', matrix, shaped, precision=lax.Precision.HIGHEST)
    return result.reshape(extent_rows, extent_cols, levels)

def along_second(values, matrix):
    extent_rows, extent_cols, levels = values.shape
    shaped = values.reshape(extent_rows, extent_cols // NP, NP, levels)
    result = jnp.einsum('ik,xekl->xeil', matrix, shaped, precision=lax.Precision.HIGHEST)
    return result.reshape(extent_rows, extent_cols, levels)

def tendency(atmos, wind_east, wind_north):
    first_order = gll_derivative()
    second_order = jnp.asarray(first_order @ first_order, jnp.float32)
    first_order = jnp.asarray(first_order, jnp.float32)
    slope_east = along_first(atmos, first_order)
    slope_north = along_second(atmos, first_order)
    curvature = along_first(atmos, second_order) + along_second(atmos, second_order)
    return viscosity * curvature - (wind_east * slope_east + wind_north * slope_north)

def pair_mean(values, after, before, axis):
    length = values.shape[axis]
    extent = [1] * values.ndim
    extent[axis] = length
    position = (jnp.arange(length, dtype=jnp.int32) % NP).reshape(extent)
    return jnp.where(position == NP - 1, 0.5 * (values + after), jnp.where(position == 0, 0.5 * (values + before), values))

def assemble(tendency_field):
    across = pair_mean(tendency_field, jnp.roll(tendency_field, -1, 0), jnp.roll(tendency_field, 1, 0), 0)
    return pair_mean(across, jnp.roll(across, -1, 1), jnp.roll(across, 1, 1), 1)

def stencil(neighbors, coupling):
    extent_rows, extent_cols = (neighbors.shape[1], neighbors.shape[2])
    row_local = (jnp.arange(extent_rows, dtype=jnp.int32) % OX)[None, :, None]
    col_local = (jnp.arange(extent_cols, dtype=jnp.int32) % OY)[None, None, :]
    offset_row = neighbors // (OY + 2) - 1 - row_local
    offset_col = neighbors % (OY + 2) - 1 - col_local
    offset_code = (offset_row + 1) * 3 + offset_col + 1
    layers = [lax.optimization_barrier(jnp.sum(jnp.where(offset_code == o, coupling, 0.0), axis=0)) for o in range(9)]
    layers[4] = layers[4] - lax.optimization_barrier(jnp.sum(coupling, axis=0))
    return jnp.stack(layers)

def spread(weights_nine, values):
    summed = jnp.zeros_like(values)
    for o in range(9):
        summed = summed + weights_nine[o] * jnp.roll(values, (1 - o // 3, 1 - o % 3), (0, 1))
    return summed

def to_blocks(values, rows_dev, cols_dev):
    shaped = values.reshape(N_COMP, rows_dev, N_TILE, cols_dev).transpose(0, 2, 1, 3)
    return shaped.reshape(N_COMP, N_TILE, rows_dev * cols_dev)

def from_blocks(blocks, rows_dev, cols_dev):
    shaped = blocks.reshape(N_COMP, N_TILE, rows_dev, cols_dev).transpose(0, 2, 1, 3)
    return shaped.reshape(N_COMP * rows_dev, N_TILE * cols_dev)

def remap(blocks, source, target, weight, cell_count):
    picked = jnp.take_along_axis(blocks, source.reshape(N_COMP, N_TILE, N_TILE * SLOT), axis=2)
    picked = picked.reshape(N_COMP, N_TILE, N_TILE, SLOT).transpose(0, 2, 1, 3)
    products = weight.reshape(N_COMP, N_TILE, N_TILE, SLOT) * picked
    device = jnp.arange(N_COMP * N_TILE, dtype=jnp.int32).reshape(N_COMP, N_TILE, 1, 1)
    flat_index = device * cell_count + target.reshape(N_COMP, N_TILE, N_TILE, SLOT)
    summed = jax.ops.segment_sum(products.reshape(-1), flat_index.reshape(-1), num_segments=N_COMP * N_TILE * cell_count)
    return summed.reshape(N_COMP, N_TILE, cell_count)

def reference(atmos_state, wind_field, ocean_height, ocean_potential, ocean_neighbors, ocean_coupling, downward_source, downward_target, downward_weight, upward_source, upward_target, upward_weight):
    atmos = atmos_state
    wind_east = wind_field[0].astype(jnp.float32)
    wind_north = wind_field[1].astype(jnp.float32)
    for substep in range(SUBSTEPS):
        tendency_field = tendency(atmos, wind_east, wind_north)
        atmos = atmos + atmos_step * assemble(tendency_field)
    surface = to_blocks(atmos[:, :, LEV - 1], AX, AY)
    forcing = from_blocks(remap(surface, downward_source, downward_target, downward_weight, OX * OY), OX, OY)
    weights_nine = stencil(ocean_neighbors, ocean_coupling)
    height = ocean_height
    potential = ocean_potential
    for substep in range(SUBCYCLES):
        potential = (1.0 - friction) * potential + ocean_step * (wave_speed * height + forcing)
        height = height + ocean_step * spread(weights_nine, potential)
    cells = to_blocks(height, OX, OY)
    surface_flux = from_blocks(remap(cells, upward_source, upward_target, upward_weight, AX * AY), AX, AY)
    return (atmos, height, potential, surface_flux)
```

```python
import jax
import jax.numpy as jnp
import numpy as np
from jax import lax
from jax.experimental import pallas as pl
from jax.experimental.pallas import tpu as pltpu
from jax.sharding import PartitionSpec as P

F32 = jnp.float32
MESH = pl.DeviceIdType.MESH
HIGHEST = lax.Precision.HIGHEST
NT = (((1,), (1,)), ((), ()))
NN = (((1,), (0,)), ((), ()))

SUBSTEPS = 2
SUBCYCLES = 8
NC = 16
NR = 64
AX, AY = 8, 16
PTS = AX * AY
OX, OY = 32, 128
ROWS = OX + 16

atmos_step = 0.05
viscosity = 0.05
ocean_step = 0.2
wave_speed = 1.0
friction = 0.05

HALO, TABLE, EDGE, OCEAN, MATRIX, GATHER, UP, FAR = 0, 1, 2, 4, 7, 10, 11, 12


def gll_derivative():
    points = np.array([-1.0, -1.0 / np.sqrt(5.0), 1.0 / np.sqrt(5.0), 1.0])
    weights = np.array(
        [1.0 / np.prod([points[j] - points[k] for k in range(4) if k != j]) for j in range(4)]
    )
    matrix = np.zeros((4, 4))
    for i in range(4):
        for j in range(4):
            if i != j:
                matrix[i, j] = weights[j] / weights[i] / (points[i] - points[j])
        matrix[i, i] = -np.sum(matrix[i])
    return matrix


def point_operators():
    first = gll_derivative()
    second = first @ first
    along_x = lambda m: np.kron(np.kron(np.eye(AX // 4), m), np.eye(AY))
    along_y = lambda m: np.kron(np.eye(AX), np.kron(np.eye(AY // 4), m))
    curvature = viscosity * (along_x(second) + along_y(second))
    return np.concatenate([curvature, along_x(first), along_y(first)]).astype(np.float32)


def iota(shape, dim):
    return lax.broadcasted_iota(jnp.int32, shape, dim)


def roll(x, shift, axis):
    return pltpu.roll(x, shift % x.shape[axis], axis)


def kernel(
    atmos_in, wind_in, height_in, potential_in, neigh_in, coup_in,
    dsrc_in, dtgt_in, dwgt_in, usrc_in, utgt_in, uwgt_in, oper_in,
    atmos_out, height_out, potential_out, flux_out,
    atmos_v, wind_v, neigh_v, coup_v, dsrc_v, dtgt_v, dwgt_v, usrc_v, utgt_v, uwgt_v, oper_v,
    surf_h, tab_s, tab_r, edge_s, edge_r, oc0, oc_pack, oc_right, oc_left,
    mx0, mx_pack, mx_right, mx_left, g_s, g_r, h_s, u_r, part_v, wst_v,
    aout_v, pout_v, fout_v, in_sem, out_sem, ssem, rsem,
):
    c = lax.axis_index("comp")
    t = lax.axis_index("tile")
    k = t % 2
    r = t // 2
    z = t // 16
    y = (t // 2) % 8
    up_row = (c + 1) % NC
    down_row = (c + NC - 1) % NC
    right = (t + 1) % NR
    left = (t + NR - 1) % NR
    own_q = k * 32 + r

    def at(dc, dt):
        row = c if dc == 0 else (up_row if dc > 0 else down_row)
        col = t if dt == 0 else (right if dt > 0 else left)
        return (row, col)

    around = [(i, j) for i in (-1, 0, 1) for j in (-1, 0, 1) if (i, j) != (0, 0)]

    def send(src, dst, which, to, left_by=None):
        pltpu.make_async_remote_copy(
            src_ref=src, dst_ref=dst,
            send_sem=ssem.at[which if left_by is None else left_by], recv_sem=rsem.at[which],
            device_id=to, device_id_type=MESH,
        ).start()

    def take(ref, sem):
        pltpu.make_async_copy(ref, ref, sem).wait()

    loads = [
        pltpu.make_async_copy(src, dst, in_sem.at[i])
        for i, (src, dst) in enumerate([
            (atmos_in, atmos_v), (oper_in, oper_v), (wind_in, wind_v),
            (dsrc_in, dsrc_v), (usrc_in, usrc_v),
            (neigh_in, neigh_v), (coup_in, coup_v),
            (height_in, oc0.at[0, pl.ds(0, OX)]), (potential_in, oc0.at[1, pl.ds(0, OX)]),
            (dtgt_in, dtgt_v), (dwgt_in, dwgt_v), (utgt_in, utgt_v), (uwgt_in, uwgt_v),
        ])
    ]
    for load in loads:
        load.start()
    surf_h[:, 9:16, :] = jnp.zeros((3, 7, PTS), F32)

    barrier = pltpu.get_barrier_semaphore()

    def greet(to):
        pl.semaphore_signal(barrier, inc=1, device_id=to, device_id_type=MESH)

    for i, j in around:
        if i != 0:
            greet(at(i, j))

    def greet_far(i, carry):
        greet((up_row, i))
        greet((down_row, 48 + i))
        return carry

    lax.fori_loop(0, 16, greet_far, 0)

    def greet_row(i, carry):
        greet((c, (t + 1 + i) % NR))
        return carry

    lax.fori_loop(0, NR - 1, greet_row, 0)

    lane8 = iota((8, 128), 1)
    last = jnp.where(lane8 == 127, 1.0, 0.0).astype(F32)
    pick_last = lambda block: lax.dot_general(
        last, block, NT, precision=HIGHEST, preferred_element_type=F32
    )[0:1]
    loads[0].wait()
    loads[1].wait()
    loads[2].wait()
    atmos = atmos_v[...]
    east = wind_v[0:PTS].astype(F32)
    north = wind_v[PTS:2 * PTS].astype(F32)
    surf_h[0, 4:5] = pick_last(atmos)
    surf_h[1, 4:5] = pick_last(east)
    surf_h[2, 4:5] = pick_last(north)

    def rate_of(a):
        res = lax.dot_general(oper_v[...], a, NN, precision=HIGHEST, preferred_element_type=F32)
        return res[0:PTS] - (east * res[PTS:2 * PTS] + north * res[2 * PTS:3 * PTS])

    def stage_edges(step, rate):
        edge_s[step, 0:16] = rate[0:16]
        edge_s[step, 16:32] = rate[112:128]
        shaped = rate.reshape(AX, AY, 128)
        edge_s[step, 32:40] = shaped[:, 0]
        edge_s[step, 40:48] = shaped[:, 15]

    def send_edges(step):
        s = lambda lo, n: edge_s.at[step, pl.ds(lo, n)]
        d = lambda lo, n: edge_r.at[step, pl.ds(lo, n)]
        which = EDGE + step
        send(s(0, 16), d(0, 16), which, at(-1, 0))
        send(s(16, 16), d(16, 16), which, at(1, 0))
        send(s(0, 1), d(48, 1), which, at(-1, -1))
        send(s(15, 1), d(49, 1), which, at(-1, 1))
        send(s(16, 1), d(50, 1), which, at(1, -1))
        send(s(31, 1), d(51, 1), which, at(1, 1))
        send(s(32, 8), d(32, 8), which, at(0, -1))
        send(s(40, 8), d(40, 8), which, at(0, 1))

    rate0 = rate_of(atmos)
    stage_edges(0, rate0)

    loads[3].wait()
    loads[4].wait()
    band = iota((NR, 128), 0)
    tab_s[0] = (dsrc_v[...] - 2 * band).astype(F32)
    tab_s[1] = (usrc_v[...] - 64 * band).astype(F32)
    for d in range(2):
        tab_r[d, pl.ds(own_q, 1)] = tab_s[d, pl.ds(t, 1)]

    for i in (5, 6, 7, 8):
        loads[i].wait()
    base = iota((OX, OY), 0) * (OY + 2) + iota((OX, OY), 1)
    links = [(neigh_v[l] - base, coup_v[l]) for l in range(6)]

    def weight_of(di, dj):
        code = (di + 1) * (OY + 2) + dj + 1
        total = jnp.zeros((OX, OY), F32)
        for place, coef in links:
            total = total + jnp.where(place == code, coef, 0.0)
        return total

    own = slice(0, OX)
    oc0[2, own] = weight_of(-1, 0)
    oc0[3, own] = weight_of(1, 0)
    oc0[4, own] = weight_of(0, -1)
    oc0[5, own] = weight_of(0, 1)
    oc0[6, own] = weight_of(1, 1) - weight_of(1, -1)
    oc0[7, own] = weight_of(-1, -1) - weight_of(-1, 1)

    lane_o = iota((OX, OY), 1)

    def pack(fields):
        packed = jnp.zeros((OX, OY), F32)
        for f, value in enumerate(fields):
            packed = jnp.where(lane_o // 8 == f, roll(value, 8 * f, 1), packed)
            packed = jnp.where(lane_o // 8 == 8 + f, roll(value, 72 + 8 * f, 1), packed)
        return packed

    def send_block(full, packed, rt, lf, which):
        top, bottom = pl.ds(0, 8), pl.ds(24, 8)
        send(full.at[:, bottom], full.at[:, pl.ds(40, 8)], which, at(1, 0))
        send(full.at[:, top], full.at[:, pl.ds(32, 8)], which, at(-1, 0))
        send(packed.at[bottom], rt.at[pl.ds(40, 8)], which + 1, at(1, -1))
        send(packed.at[top], rt.at[pl.ds(32, 8)], which + 1, at(-1, -1))
        send(packed, rt.at[pl.ds(0, OX)], which + 1, at(0, -1))
        send(packed.at[bottom], lf.at[pl.ds(40, 8)], which + 2, at(1, 1))
        send(packed.at[top], lf.at[pl.ds(32, 8)], which + 2, at(-1, 1))
        send(packed, lf.at[pl.ds(0, OX)], which + 2, at(0, 1))

    def take_block(full, rt, lf, sems, which):
        take(full.at[:, pl.ds(32, 16)], sems.at[which])
        take(rt, sems.at[which + 1])
        take(lf, sems.at[which + 2])

    lane_x = iota((ROWS, OY), 1)

    def beside(rt, lf, f):
        from_right = roll(rt, -8 * f, 1)
        from_left = roll(lf, 56 - 8 * f, 1)
        return jnp.where(lane_x < 8, from_right, jnp.where(lane_x >= 120, from_left, 0.0))

    oc_pack[...] = pack([oc0[f, own] for f in range(8)])

    far = jnp.where((z == 0) | (z == 3), 1, 0)
    pl.semaphore_wait(barrier, NR - 1 + 6 + NR * far)

    centre = pl.ds(4, 1)
    for i, j in around:
        send(surf_h.at[:, centre], surf_h.at[:, pl.ds(4 - 3 * i - j, 1)], HALO, at(i, j))

    def ordered(i):
        j = i // 8
        step_y = 4 + ((j + 1) // 2) * (2 * (j % 2) - 1)
        zk = (i + 1) % 8
        return ((z + zk // 2) % 4) * 16 + ((y + step_y) % 8) * 2 + (k + zk) % 2

    def send_table(i, carry):
        to = ordered(i)
        send(tab_s.at[:, pl.ds(to, 1)], tab_r.at[:, pl.ds(own_q, 1)], TABLE, (c, to))
        return carry

    lax.fori_loop(0, NR - 1, send_table, 0)
    send_edges(0)
    send_block(oc0, oc_pack, oc_right, oc_left, OCEAN)

    lane_s = iota((16, PTS), 1)
    xs, ys = lane_s // AY, lane_s % AY

    def pairs(values, after, before, pos):
        return jnp.where(
            pos == 3, 0.5 * (values + after), jnp.where(pos == 0, 0.5 * (values + before), values)
        )

    take(edge_r.at[0, pl.ds(0, 24)], rsem.at[HALO])
    surf = surf_h[0]
    surf_e = surf_h[1]
    surf_n = surf_h[2]
    for _ in range(SUBSTEPS):
        res = lax.dot_general(surf, oper_v[...], NT, precision=HIGHEST, preferred_element_type=F32)
        rate = res[:, 0:PTS] - (surf_e * res[:, PTS:2 * PTS] + surf_n * res[:, 2 * PTS:3 * PTS])
        nxt, prv = roll(rate, -16, 1), roll(rate, 16, 1)
        after = jnp.where(xs == AX - 1, roll(nxt, -3, 0), nxt)
        before = jnp.where(xs == 0, roll(prv, 3, 0), prv)
        rate = pairs(rate, after, before, xs % 4)
        after = jnp.where(ys == AY - 1, roll(roll(rate, 15, 1), -1, 0), roll(rate, -1, 1))
        before = jnp.where(ys == 0, roll(roll(rate, -15, 1), 1, 0), roll(rate, 1, 1))
        surf = surf + atmos_step * pairs(rate, after, before, ys % 4)
    surf_row = surf[4:5]
    g_s[0:1] = surf_row
    g_r[pl.ds(k * ROWS + r, 1)] = surf_row

    @pl.when(far == 1)
    def _():
        row = jnp.where(z == 0, down_row, up_row)
        place = k * ROWS + jnp.where(z == 0, 32, 40) + y

        def send_far(i, carry):
            send(g_s.at[pl.ds(0, 1)], g_r.at[pl.ds(place, 1)], GATHER, (row, ordered(i)), FAR)
            return carry

        lax.fori_loop(0, NR, send_far, 0)

    def send_surface(i, carry):
        send(g_s.at[pl.ds(0, 1)], g_r.at[pl.ds(k * ROWS + r, 1)], GATHER, (c, ordered(i)))
        return carry

    lax.fori_loop(0, NR - 1, send_surface, 0)

    row_q = iota((NR, 128), 0)
    peer_q = 2 * (row_q % 32) + row_q // 32
    lane_64 = iota((NR, 128), 1)

    def by_core(ref):
        return jnp.concatenate(
            [ref[pl.ds(0, 32, stride=2), :], ref[pl.ds(1, 32, stride=2), :]], axis=0
        )

    def turned(value):
        tall = jnp.concatenate([value, jnp.zeros((128 - NR, 128), F32)], axis=0).T
        return jnp.where(lane_64 < 64, tall[0:64], roll(tall[64:128], 64, 1))

    def matrices(cell, second, weight):
        cell_t = turned(cell)
        one = weight * second
        one_t = turned(one)
        zero_t = turned(weight - one)

        def group(g, carry):
            for i in range(8):
                n = g * 8 + i
                hit = cell_t == n.astype(F32)
                part_v[0, pl.ds(n, 1)] = jnp.sum(jnp.where(hit, zero_t, 0.0), axis=0, keepdims=True)
                part_v[1, pl.ds(n, 1)] = jnp.sum(jnp.where(hit, one_t, 0.0), axis=0, keepdims=True)
            return carry

        lax.fori_loop(0, 8, group, 0)
        return [part_v[j] + roll(part_v[j], 64, 1) for j in range(2)]

    for i in (9, 10):
        loads[i].wait()
    take(tab_r.at[:, pl.ds(0, NR - 1)], rsem.at[TABLE])
    down = matrices(
        (by_core(dtgt_v) - 64 * peer_q).astype(F32), tab_r[0], by_core(dwgt_v)
    )
    for j in range(2):
        cells = jnp.concatenate([down[j], roll(down[j], -32, 1)], axis=0).T
        mx0[j, own] = cells[0:OX]
    mx_pack[...] = pack([mx0[j, own] for j in range(2)])
    send_block(mx0, mx_pack, mx_right, mx_left, MATRIX)

    row_a = iota((PTS, 128), 0)
    xa, ya = row_a // AY, row_a % AY
    row_e = iota((AX, 128), 0)

    def finish(step, a, rate):
        take(edge_r.at[step, pl.ds(0, 52)], rsem.at[EDGE + step])
        recv = lambda lo, n: edge_r[step, lo:lo + n]
        after = jnp.concatenate([rate[16:128], recv(0, 16)], axis=0)
        before = jnp.concatenate([recv(16, 16), rate[0:112]], axis=0)
        across = pairs(rate, after, before, xa % 4)

        def column(lo, beyond, ahead):
            col = recv(lo, 8)
            nxt = jnp.where(row_e == 7, beyond, roll(col, -1, 0))
            prv = jnp.where(row_e == 0, ahead, roll(col, 1, 0))
            col = pairs(col, nxt, prv, row_e % 4)
            return jnp.broadcast_to(col[:, None, :], (AX, AY, 128)).reshape(PTS, 128)

        east_col = column(32, recv(48, 1), recv(50, 1))
        west_col = column(40, recv(49, 1), recv(51, 1))
        after = jnp.where(ya == AY - 1, east_col, roll(across, -1, 0))
        before = jnp.where(ya == 0, west_col, roll(across, 1, 0))
        return a + atmos_step * pairs(across, after, before, ya % 4)

    atmos = finish(0, atmos, rate0)
    rate1 = rate_of(atmos)
    stage_edges(1, rate1)
    send_edges(1)

    for i in (11, 12):
        loads[i].wait()
    upward = matrices(
        tab_r[1], (by_core(utgt_v) - 2 * peer_q).astype(F32), by_core(uwgt_v)
    )
    up_cells = []
    blank = jnp.zeros((NR, 128), F32)
    for j in range(2):
        low = jnp.where(k == 0, upward[j], blank)
        high = jnp.where(k == 0, blank, upward[j])
        up_cells.append(jnp.concatenate([low, high], axis=0).T[0:NR])

    take_block(oc0, oc_right, oc_left, rsem, OCEAN)
    oc_rt, oc_lf = oc_right[...], oc_left[...]
    wide = [jnp.concatenate([oc0[f], beside(oc_rt, oc_lf, f)], axis=1) for f in range(8)]
    height, potential, w_n, w_s, w_w, w_e, pair_s, pair_n = wide
    w_se, w_sw = jnp.maximum(pair_s, 0.0), jnp.maximum(-pair_s, 0.0)
    w_nw, w_ne = jnp.maximum(pair_n, 0.0), jnp.maximum(-pair_n, 0.0)
    w_c = -(w_n + w_s + w_w + w_e + w_se + w_sw + w_nw + w_ne)
    for i, (value, shift) in enumerate([
        (w_nw, -1), (w_w, -1), (w_sw, -1),
        (w_n, 0), (w_c, 0), (w_s, 0),
        (w_ne, 1), (w_e, 1), (w_se, 1),
    ]):
        value = ocean_step * value
        wst_v[i] = value if shift == 0 else roll(value, shift, 1)

    atmos = finish(1, atmos, rate1)
    aout_v[...] = atmos
    atmos_copy = pltpu.make_async_copy(aout_v, atmos_out, out_sem.at[0])
    atmos_copy.start()

    take_block(mx0, mx_right, mx_left, rsem, MATRIX)
    mx_rt, mx_lf = mx_right[...], mx_left[...]
    mx1 = [beside(mx_rt, mx_lf, j) for j in range(2)]
    take(g_r.at[pl.ds(0, 95)], rsem.at[GATHER])
    even, odd = g_r[0:ROWS], g_r[ROWS:2 * ROWS]

    def column_of(block, point):
        return jnp.sum(jnp.where(lane_x == point, block, 0.0), axis=1, keepdims=True)

    near = jnp.zeros((ROWS, OY), F32)
    side = jnp.zeros((ROWS, OY), F32)
    for j in range(2):
        here = jnp.where(lane_x < 64, column_of(even, 2 * t + j), column_of(odd, 2 * t + j))
        there = jnp.where(
            lane_x < 64, column_of(even, 2 * right + j), column_of(odd, 2 * left + j)
        )
        near = near + mx0[j] * here
        side = side + mx1[j] * there
    forcing = ocean_step * jnp.concatenate([near, side], axis=1)

    for _ in range(SUBCYCLES):
        potential = (1.0 - friction) * potential + (ocean_step * wave_speed) * height + forcing
        above = roll(potential, 1, 0)
        below = roll(potential, -1, 0)
        sums = [
            wst_v[3 * j] * above + wst_v[3 * j + 1] * potential + wst_v[3 * j + 2] * below
            for j in range(3)
        ]
        height = height + sums[1] + roll(sums[0], 1, 1) + roll(sums[2], -1, 1)

    h_s[...] = height[0:OX, 0:OY]
    u_r[pl.ds(own_q, 1)] = h_s[pl.ds(r, 1)]

    def send_height(i, carry):
        to = ordered(i)
        send(h_s.at[pl.ds(to // 2, 1)], u_r.at[pl.ds(own_q, 1)], UP, (c, to))
        return carry

    lax.fori_loop(0, NR - 1, send_height, 0)
    pout_v[...] = potential[0:OX, 0:OY]
    height_copy = pltpu.make_async_copy(h_s, height_out, out_sem.at[1])
    potential_copy = pltpu.make_async_copy(pout_v, potential_out, out_sem.at[2])
    height_copy.start()
    potential_copy.start()

    take(edge_r.at[0, pl.ds(0, 24)], ssem.at[HALO])
    take(tab_r.at[:, pl.ds(0, NR - 1)], ssem.at[TABLE])
    take(edge_r.at[0, pl.ds(0, 52)], ssem.at[EDGE])
    take(edge_r.at[1, pl.ds(0, 52)], ssem.at[EDGE + 1])
    take_block(oc0, oc_right, oc_left, ssem, OCEAN)
    take_block(mx0, mx_right, mx_left, ssem, MATRIX)
    take(g_r.at[pl.ds(0, NR - 1)], ssem.at[GATHER])

    @pl.when(far == 1)
    def _():
        take(g_r.at[pl.ds(0, NR)], ssem.at[FAR])

    q_row = iota((AX, NR), 1)
    pick = jnp.where((q_row % 32) // 4 == iota((AX, NR), 0), 1.0, 0.0).astype(F32)
    column0 = 4 * (row_q % 4) + 2 * (row_q // 32)
    take(u_r.at[pl.ds(0, NR - 1)], rsem.at[UP])
    cells = u_r[...]
    spread = jnp.zeros((NR, 128), F32)
    for j in range(2):
        total = jnp.sum(up_cells[j] * cells, axis=1, keepdims=True)
        spread = spread + jnp.where(lane_64 == column0 + j, total, 0.0)
    flux = lax.dot_general(pick, spread, NN, precision=HIGHEST, preferred_element_type=F32)
    fout_v[...] = flux[:, 0:AY]
    flux_copy = pltpu.make_async_copy(fout_v, flux_out, out_sem.at[3])
    flux_copy.start()
    take(u_r.at[pl.ds(0, NR - 1)], ssem.at[UP])
    for copy in (atmos_copy, height_copy, potential_copy, flux_copy):
        copy.wait()


def on_device(
    atmos_state, wind_field, ocean_height, ocean_potential, ocean_neighbors, ocean_coupling,
    downward_source, downward_target, downward_weight,
    upward_source, upward_target, upward_weight,
):
    table = lambda value: value.reshape(NR, 128)
    any_spec = pl.BlockSpec(memory_space=pl.ANY)
    vm = lambda *shape, dtype=F32: pltpu.VMEM(shape, dtype)
    i32 = jnp.int32
    outs = pl.pallas_call(
        kernel,
        out_shape=[
            jax.ShapeDtypeStruct((PTS, 128), F32),
            jax.ShapeDtypeStruct((OX, OY), F32),
            jax.ShapeDtypeStruct((OX, OY), F32),
            jax.ShapeDtypeStruct((AX, AY), F32),
        ],
        in_specs=[any_spec] * 13,
        out_specs=[any_spec] * 4,
        scratch_shapes=[
            vm(PTS, 128), vm(2 * PTS, 128, dtype=jnp.bfloat16),
            vm(6, OX, OY, dtype=i32), vm(6, OX, OY),
            vm(NR, 128, dtype=i32), vm(NR, 128, dtype=i32), vm(NR, 128),
            vm(NR, 128, dtype=i32), vm(NR, 128, dtype=i32), vm(NR, 128),
            vm(3 * PTS, PTS),
            vm(3, 16, PTS), vm(2, NR, 128), vm(2, NR, 128), vm(2, 48, 128), vm(2, 56, 128),
            vm(8, ROWS, OY), vm(OX, OY), vm(ROWS, OY), vm(ROWS, OY),
            vm(2, ROWS, OY), vm(OX, OY), vm(ROWS, OY), vm(ROWS, OY),
            vm(8, 128), vm(2 * ROWS, 128), vm(OX, OY), vm(NR, 128),
            vm(2, NR, 128), vm(9, ROWS, 256),
            vm(PTS, 128), vm(OX, OY), vm(AX, AY),
            pltpu.SemaphoreType.DMA((13,)), pltpu.SemaphoreType.DMA((4,)),
            pltpu.SemaphoreType.DMA((13,)), pltpu.SemaphoreType.DMA((12,)),
        ],
        compiler_params=pltpu.CompilerParams(
            collective_id=0, has_side_effects=True, vmem_limit_bytes=60 * 1024 * 1024
        ),
        name="coupled_step",
    )(
        atmos_state.reshape(PTS, 128), wind_field.reshape(2 * PTS, 128),
        ocean_height, ocean_potential, ocean_neighbors, ocean_coupling,
        table(downward_source), table(downward_target), table(downward_weight),
        table(upward_source), table(upward_target), table(upward_weight),
        jnp.asarray(point_operators()),
    )
    return (outs[0].reshape(AX, AY, 128), outs[1], outs[2], outs[3])


def solution(mesh):
    cells = P(None, "comp", "tile")
    tables = P("comp", "tile", None)
    flat = P("comp", "tile")
    return jax.shard_map(
        on_device,
        mesh=mesh,
        in_specs=(tables, P(None, "comp", "tile", None), flat, flat, cells, cells) + (tables,) * 6,
        out_specs=(tables, flat, flat, flat),
        check_vma=False,
    )
```

```python
import jax
import jax.numpy as jnp
import numpy as np
from jax import lax
from jax.experimental import pallas as pl
from jax.experimental.pallas import tpu as pltpu
from jax.sharding import PartitionSpec as P

F32 = jnp.float32
MESH = pl.DeviceIdType.MESH
HIGHEST = lax.Precision.HIGHEST
NT = (((1,), (1,)), ((), ()))
NN = (((1,), (0,)), ((), ()))

SUBSTEPS = 2
SUBCYCLES = 8
NC = 16
NR = 64
AX, AY = 8, 16
PTS = AX * AY
OX, OY = 32, 128
ROWS = OX + 16

atmos_step = 0.05
viscosity = 0.05
ocean_step = 0.2
wave_speed = 1.0
friction = 0.05

HALO, TABLE, EDGE, OCEAN, MATRIX, GATHER, UP, FAR = 0, 1, 2, 4, 7, 10, 11, 12


def gll_derivative():
    points = np.array([-1.0, -1.0 / np.sqrt(5.0), 1.0 / np.sqrt(5.0), 1.0])
    weights = np.array(
        [1.0 / np.prod([points[j] - points[k] for k in range(4) if k != j]) for j in range(4)]
    )
    matrix = np.zeros((4, 4))
    for i in range(4):
        for j in range(4):
            if i != j:
                matrix[i, j] = weights[j] / weights[i] / (points[i] - points[j])
        matrix[i, i] = -np.sum(matrix[i])
    return matrix


def point_operators():
    first = gll_derivative()
    second = first @ first
    along_x = lambda m: np.kron(np.kron(np.eye(AX // 4), m), np.eye(AY))
    along_y = lambda m: np.kron(np.eye(AX), np.kron(np.eye(AY // 4), m))
    curvature = viscosity * (along_x(second) + along_y(second))
    return np.concatenate([curvature, along_x(first), along_y(first)]).astype(np.float32)


def iota(shape, dim):
    return lax.broadcasted_iota(jnp.int32, shape, dim)


def roll(x, shift, axis):
    return pltpu.roll(x, shift % x.shape[axis], axis)


def kernel(
    atmos_in, wind_in, height_in, potential_in, neigh_in, coup_in,
    dsrc_in, dtgt_in, dwgt_in, usrc_in, utgt_in, uwgt_in, oper_in,
    result,
    atmos_v, wind_v, neigh_v, coup_v, dsrc_v, dtgt_v, dwgt_v, usrc_v, utgt_v, uwgt_v, oper_v,
    surf_h, tab_s, tab_r, edge_s, edge_r, oc0, oc_pack, oc_right, oc_left,
    mx0, mx_pack, mx_right, mx_left, g_s, g_r, h_s, u_r, part_v, wst_v,
    in_sem, ssem, rsem,
):
    c = lax.axis_index("comp")
    t = lax.axis_index("tile")
    k = t % 2
    r = t // 2
    z = t // 16
    y = (t // 2) % 8
    up_row = (c + 1) % NC
    down_row = (c + NC - 1) % NC
    right = (t + 1) % NR
    left = (t + NR - 1) % NR
    own_q = k * 32 + r

    wrap = lambda value, size: jnp.where(value >= size, value - size, value)
    over_y = [wrap(y + i, 8) for i in (4, 5, 3, 6, 2, 7, 1, 0)]
    over_z = [8 * wrap(z + i, 4) for i in (2, 1, 3, 0)]
    chips = [zz + yy for yy in over_y for zz in over_z]
    row_order = [2 * chip + kk for chip in chips for kk in (1 - k, k)]
    peers = row_order[:-1]
    peer_chips = [chip for chip in chips for _ in range(2)][:-1]

    def at(dc, dt):
        row = c if dc == 0 else (up_row if dc > 0 else down_row)
        col = t if dt == 0 else (right if dt > 0 else left)
        return (row, col)

    around = [(i, j) for i in (-1, 0, 1) for j in (-1, 0, 1) if (i, j) != (0, 0)]

    def send(src, dst, which, to, left_by=None):
        pltpu.make_async_remote_copy(
            src_ref=src, dst_ref=dst,
            send_sem=ssem.at[which if left_by is None else left_by], recv_sem=rsem.at[which],
            device_id=to, device_id_type=MESH,
        ).start()

    def take(ref, sem):
        pltpu.make_async_copy(ref, ref, sem).wait()

    loads = [
        pltpu.make_async_copy(src, dst, in_sem.at[i])
        for i, (src, dst) in enumerate([
            (atmos_in, atmos_v), (oper_in, oper_v), (wind_in, wind_v),
            (dsrc_in, dsrc_v), (usrc_in, usrc_v),
            (neigh_in, neigh_v), (coup_in, coup_v),
            (height_in, oc0.at[0, pl.ds(0, OX)]), (potential_in, oc0.at[1, pl.ds(0, OX)]),
            (dtgt_in, dtgt_v), (dwgt_in, dwgt_v), (utgt_in, utgt_v), (uwgt_in, uwgt_v),
        ])
    ]
    for load in loads:
        load.start()
    surf_h[:, 9:16, :] = jnp.zeros((3, 7, PTS), F32)

    barrier = pltpu.get_barrier_semaphore()

    def greet(to):
        pl.semaphore_signal(barrier, inc=1, device_id=to, device_id_type=MESH)

    for i, j in around:
        if i != 0:
            greet(at(i, j))

    for i in range(16):
        greet((up_row, i))
        greet((down_row, 48 + i))
    for to in peers:
        greet((c, to))

    lane8 = iota((8, 128), 1)
    last = jnp.where(lane8 == 127, 1.0, 0.0).astype(F32)
    pick_last = lambda block: lax.dot_general(
        last, block, NT, precision=HIGHEST, preferred_element_type=F32
    )[0:1]
    loads[0].wait()
    loads[1].wait()
    loads[2].wait()
    atmos = atmos_v[...]
    east = wind_v[0:PTS].astype(F32)
    north = wind_v[PTS:2 * PTS].astype(F32)
    surf_h[0, 4:5] = pick_last(atmos)
    surf_h[1, 4:5] = pick_last(east)
    surf_h[2, 4:5] = pick_last(north)

    def rate_of(a):
        res = lax.dot_general(oper_v[...], a, NN, precision=HIGHEST, preferred_element_type=F32)
        return res[0:PTS] - (east * res[PTS:2 * PTS] + north * res[2 * PTS:3 * PTS])

    def stage_edges(step, rate):
        edge_s[step, 0:16] = rate[0:16]
        edge_s[step, 16:32] = rate[112:128]
        shaped = rate.reshape(AX, AY, 128)
        edge_s[step, 32:40] = shaped[:, 0]
        edge_s[step, 40:48] = shaped[:, 15]

    def send_edges(step):
        s = lambda lo, n: edge_s.at[step, pl.ds(lo, n)]
        d = lambda lo, n: edge_r.at[step, pl.ds(lo, n)]
        which = EDGE + step
        send(s(0, 16), d(0, 16), which, at(-1, 0))
        send(s(16, 16), d(16, 16), which, at(1, 0))
        send(s(0, 1), d(48, 1), which, at(-1, -1))
        send(s(15, 1), d(49, 1), which, at(-1, 1))
        send(s(16, 1), d(50, 1), which, at(1, -1))
        send(s(31, 1), d(51, 1), which, at(1, 1))
        send(s(32, 8), d(32, 8), which, at(0, -1))
        send(s(40, 8), d(40, 8), which, at(0, 1))

    loads[3].wait()
    loads[4].wait()
    band = iota((NR, 128), 0)
    tab_s[0] = (dsrc_v[...] - 2 * band).astype(F32)
    tab_s[1] = (usrc_v[...] - 64 * band).astype(F32)
    for d in range(2):
        tab_r[d, pl.ds(own_q, 1)] = tab_s[d, pl.ds(t, 1)]

    far = jnp.where((z == 0) | (z == 3), 1, 0)
    pl.semaphore_wait(barrier, NR - 1 + 6 + NR * far)

    centre = pl.ds(4, 1)
    for i, j in around:
        send(surf_h.at[:, centre], surf_h.at[:, pl.ds(4 - 3 * i - j, 1)], HALO, at(i, j))

    for to in peers:
        send(tab_s.at[:, pl.ds(to, 1)], tab_r.at[:, pl.ds(own_q, 1)], TABLE, (c, to))
    rate0 = rate_of(atmos)
    stage_edges(0, rate0)

    send_edges(0)

    for i in (5, 6, 7, 8):
        loads[i].wait()
    base = iota((OX, OY), 0) * (OY + 2) + iota((OX, OY), 1)
    links = [(neigh_v[l] - base, coup_v[l]) for l in range(6)]

    def weight_of(di, dj):
        code = (di + 1) * (OY + 2) + dj + 1
        total = jnp.zeros((OX, OY), F32)
        for place, coef in links:
            total = total + jnp.where(place == code, coef, 0.0)
        return total

    own = slice(0, OX)
    oc0[2, own] = weight_of(-1, 0)
    oc0[3, own] = weight_of(1, 0)
    oc0[4, own] = weight_of(0, -1)
    oc0[5, own] = weight_of(0, 1)
    oc0[6, own] = weight_of(1, 1) - weight_of(1, -1)
    oc0[7, own] = weight_of(-1, -1) - weight_of(-1, 1)

    lane_o = iota((OX, OY), 1)

    def pack(fields):
        packed = jnp.zeros((OX, OY), F32)
        for f, value in enumerate(fields):
            packed = jnp.where(lane_o // 8 == f, roll(value, 8 * f, 1), packed)
            packed = jnp.where(lane_o // 8 == 8 + f, roll(value, 72 + 8 * f, 1), packed)
        return packed

    def send_block(full, packed, rt, lf, which):
        top, bottom = pl.ds(0, 8), pl.ds(24, 8)
        send(full.at[:, bottom], full.at[:, pl.ds(40, 8)], which, at(1, 0))
        send(full.at[:, top], full.at[:, pl.ds(32, 8)], which, at(-1, 0))
        send(packed.at[bottom], rt.at[pl.ds(40, 8)], which + 1, at(1, -1))
        send(packed.at[top], rt.at[pl.ds(32, 8)], which + 1, at(-1, -1))
        send(packed, rt.at[pl.ds(0, OX)], which + 1, at(0, -1))
        send(packed.at[bottom], lf.at[pl.ds(40, 8)], which + 2, at(1, 1))
        send(packed.at[top], lf.at[pl.ds(32, 8)], which + 2, at(-1, 1))
        send(packed, lf.at[pl.ds(0, OX)], which + 2, at(0, 1))

    def take_block(full, rt, lf, sems, which):
        take(full.at[:, pl.ds(32, 16)], sems.at[which])
        take(rt, sems.at[which + 1])
        take(lf, sems.at[which + 2])

    lane_x = iota((ROWS, OY), 1)

    def beside(rt, lf, f):
        from_right = roll(rt, -8 * f, 1)
        from_left = roll(lf, 56 - 8 * f, 1)
        return jnp.where(lane_x < 8, from_right, jnp.where(lane_x >= 120, from_left, 0.0))

    oc_pack[...] = pack([oc0[f, own] for f in range(8)])

    send_block(oc0, oc_pack, oc_right, oc_left, OCEAN)

    lane_s = iota((16, PTS), 1)
    xs, ys = lane_s // AY, lane_s % AY

    def pairs(values, after, before, pos):
        return jnp.where(
            pos == 3, 0.5 * (values + after), jnp.where(pos == 0, 0.5 * (values + before), values)
        )

    take(edge_r.at[0, pl.ds(0, 24)], rsem.at[HALO])
    surf = surf_h[0]
    surf_e = surf_h[1]
    surf_n = surf_h[2]
    for _ in range(SUBSTEPS):
        res = lax.dot_general(surf, oper_v[...], NT, precision=HIGHEST, preferred_element_type=F32)
        rate = res[:, 0:PTS] - (surf_e * res[:, PTS:2 * PTS] + surf_n * res[:, 2 * PTS:3 * PTS])
        nxt, prv = roll(rate, -16, 1), roll(rate, 16, 1)
        after = jnp.where(xs == AX - 1, roll(nxt, -3, 0), nxt)
        before = jnp.where(xs == 0, roll(prv, 3, 0), prv)
        rate = pairs(rate, after, before, xs % 4)
        after = jnp.where(ys == AY - 1, roll(roll(rate, 15, 1), -1, 0), roll(rate, -1, 1))
        before = jnp.where(ys == 0, roll(roll(rate, -15, 1), 1, 0), roll(rate, 1, 1))
        surf = surf + atmos_step * pairs(rate, after, before, ys % 4)
    surf_row = surf[4:5]
    g_s[0:1] = surf_row
    g_r[pl.ds(k * ROWS + r, 1)] = surf_row

    @pl.when(far == 1)
    def _():
        row = jnp.where(z == 0, down_row, up_row)
        place = k * ROWS + jnp.where(z == 0, 32, 40) + y

        for to in row_order:
            send(g_s.at[pl.ds(0, 1)], g_r.at[pl.ds(place, 1)], GATHER, (row, to), FAR)

    own_place = k * ROWS + r
    for to in peers:
        send(g_s.at[pl.ds(0, 1)], g_r.at[pl.ds(own_place, 1)], GATHER, (c, to))

    row_q = iota((NR, 128), 0)
    peer_q = 2 * (row_q % 32) + row_q // 32
    lane_64 = iota((NR, 128), 1)

    def by_core(ref):
        return jnp.concatenate(
            [ref[pl.ds(0, 32, stride=2), :], ref[pl.ds(1, 32, stride=2), :]], axis=0
        )

    def turned(value):
        tall = jnp.concatenate([value, jnp.zeros((128 - NR, 128), F32)], axis=0).T
        return jnp.where(lane_64 < 64, tall[0:64], roll(tall[64:128], 64, 1))

    def matrices(cell, second, weight):
        cell_t = turned(cell)
        one = weight * second
        one_t = turned(one)
        zero_t = turned(weight - one)

        def group(g, carry):
            for i in range(8):
                n = g * 8 + i
                hit = cell_t == n.astype(F32)
                part_v[0, pl.ds(n, 1)] = jnp.sum(jnp.where(hit, zero_t, 0.0), axis=0, keepdims=True)
                part_v[1, pl.ds(n, 1)] = jnp.sum(jnp.where(hit, one_t, 0.0), axis=0, keepdims=True)
            return carry

        lax.fori_loop(0, 8, group, 0)
        return [part_v[j] + roll(part_v[j], 64, 1) for j in range(2)]

    for i in (9, 10):
        loads[i].wait()
    take(tab_r.at[:, pl.ds(0, NR - 1)], rsem.at[TABLE])
    down = matrices(
        (by_core(dtgt_v) - 64 * peer_q).astype(F32), tab_r[0], by_core(dwgt_v)
    )
    for j in range(2):
        cells = jnp.concatenate([down[j], roll(down[j], -32, 1)], axis=0).T
        mx0[j, own] = cells[0:OX]
    mx_pack[...] = pack([mx0[j, own] for j in range(2)])
    send_block(mx0, mx_pack, mx_right, mx_left, MATRIX)

    row_a = iota((PTS, 128), 0)
    xa, ya = row_a // AY, row_a % AY
    row_e = iota((AX, 128), 0)

    def finish(step, a, rate):
        take(edge_r.at[step, pl.ds(0, 52)], rsem.at[EDGE + step])
        recv = lambda lo, n: edge_r[step, lo:lo + n]
        after = jnp.concatenate([rate[16:128], recv(0, 16)], axis=0)
        before = jnp.concatenate([recv(16, 16), rate[0:112]], axis=0)
        across = pairs(rate, after, before, xa % 4)

        def column(lo, beyond, ahead):
            col = recv(lo, 8)
            nxt = jnp.where(row_e == 7, beyond, roll(col, -1, 0))
            prv = jnp.where(row_e == 0, ahead, roll(col, 1, 0))
            col = pairs(col, nxt, prv, row_e % 4)
            return jnp.broadcast_to(col[:, None, :], (AX, AY, 128)).reshape(PTS, 128)

        east_col = column(32, recv(48, 1), recv(50, 1))
        west_col = column(40, recv(49, 1), recv(51, 1))
        after = jnp.where(ya == AY - 1, east_col, roll(across, -1, 0))
        before = jnp.where(ya == 0, west_col, roll(across, 1, 0))
        return a + atmos_step * pairs(across, after, before, ya % 4)

    atmos = finish(0, atmos, rate0)
    rate1 = rate_of(atmos)
    stage_edges(1, rate1)
    send_edges(1)

    for i in (11, 12):
        loads[i].wait()
    upward = matrices(
        tab_r[1], (by_core(utgt_v) - 2 * peer_q).astype(F32), by_core(uwgt_v)
    )
    up_cells = []
    blank = jnp.zeros((NR, 128), F32)
    for j in range(2):
        low = jnp.where(k == 0, upward[j], blank)
        high = jnp.where(k == 0, blank, upward[j])
        up_cells.append(jnp.concatenate([low, high], axis=0).T[0:NR])

    take_block(oc0, oc_right, oc_left, rsem, OCEAN)
    oc_rt, oc_lf = oc_right[...], oc_left[...]
    wide = [jnp.concatenate([oc0[f], beside(oc_rt, oc_lf, f)], axis=1) for f in range(8)]
    height, potential, w_n, w_s, w_w, w_e, pair_s, pair_n = wide
    w_se, w_sw = jnp.maximum(pair_s, 0.0), jnp.maximum(-pair_s, 0.0)
    w_nw, w_ne = jnp.maximum(pair_n, 0.0), jnp.maximum(-pair_n, 0.0)
    w_c = -(w_n + w_s + w_w + w_e + w_se + w_sw + w_nw + w_ne)
    for i, (value, shift) in enumerate([
        (w_nw, -1), (w_w, -1), (w_sw, -1),
        (w_n, 0), (w_c, 0), (w_s, 0),
        (w_ne, 1), (w_e, 1), (w_se, 1),
    ]):
        value = ocean_step * value
        wst_v[i] = value if shift == 0 else roll(value, shift, 1)

    atmos = finish(1, atmos, rate1)
    result[0:PTS] = atmos

    take_block(mx0, mx_right, mx_left, rsem, MATRIX)
    mx_rt, mx_lf = mx_right[...], mx_left[...]
    mx1 = [beside(mx_rt, mx_lf, j) for j in range(2)]
    take(g_r.at[pl.ds(0, 95)], rsem.at[GATHER])
    even, odd = g_r[0:ROWS], g_r[ROWS:2 * ROWS]

    def column_of(block, point):
        return jnp.sum(jnp.where(lane_x == point, block, 0.0), axis=1, keepdims=True)

    near = jnp.zeros((ROWS, OY), F32)
    side = jnp.zeros((ROWS, OY), F32)
    for j in range(2):
        here = jnp.where(lane_x < 64, column_of(even, 2 * t + j), column_of(odd, 2 * t + j))
        there = jnp.where(
            lane_x < 64, column_of(even, 2 * right + j), column_of(odd, 2 * left + j)
        )
        near = near + mx0[j] * here
        side = side + mx1[j] * there
    forcing = ocean_step * jnp.concatenate([near, side], axis=1)

    for _ in range(SUBCYCLES):
        potential = (1.0 - friction) * potential + (ocean_step * wave_speed) * height + forcing
        above = roll(potential, 1, 0)
        below = roll(potential, -1, 0)
        sums = [
            wst_v[3 * j] * above + wst_v[3 * j + 1] * potential + wst_v[3 * j + 2] * below
            for j in range(3)
        ]
        height = height + sums[1] + roll(sums[0], 1, 1) + roll(sums[2], -1, 1)

    h_s[...] = height[0:OX, 0:OY]
    u_r[pl.ds(own_q, 1)] = h_s[pl.ds(r, 1)]

    for to, chip in zip(peers, peer_chips):
        send(h_s.at[pl.ds(chip, 1)], u_r.at[pl.ds(own_q, 1)], UP, (c, to))
    result[PTS:PTS + OX] = height[0:OX, 0:OY]
    result[PTS + OX:PTS + 2 * OX] = potential[0:OX, 0:OY]

    take(edge_r.at[0, pl.ds(0, 24)], ssem.at[HALO])
    take(tab_r.at[:, pl.ds(0, NR - 1)], ssem.at[TABLE])
    take(edge_r.at[0, pl.ds(0, 52)], ssem.at[EDGE])
    take(edge_r.at[1, pl.ds(0, 52)], ssem.at[EDGE + 1])
    take_block(oc0, oc_right, oc_left, ssem, OCEAN)
    take_block(mx0, mx_right, mx_left, ssem, MATRIX)
    take(g_r.at[pl.ds(0, NR - 1)], ssem.at[GATHER])

    @pl.when(far == 1)
    def _():
        take(g_r.at[pl.ds(0, NR)], ssem.at[FAR])

    q_row = iota((AX, NR), 1)
    pick = jnp.where((q_row % 32) // 4 == iota((AX, NR), 0), 1.0, 0.0).astype(F32)
    column0 = 4 * (row_q % 4) + 2 * (row_q // 32)
    take(u_r.at[pl.ds(0, NR - 1)], rsem.at[UP])
    cells = u_r[...]
    spread = jnp.zeros((NR, 128), F32)
    for j in range(2):
        total = jnp.sum(up_cells[j] * cells, axis=1, keepdims=True)
        spread = spread + jnp.where(lane_64 == column0 + j, total, 0.0)
    flux = lax.dot_general(pick, spread, NN, precision=HIGHEST, preferred_element_type=F32)
    result[PTS + 2 * OX:PTS + 2 * OX + AX] = flux
    take(u_r.at[pl.ds(0, NR - 1)], ssem.at[UP])


def hand_out(result, atmos_out, height_out, potential_out, flux_out, flux_v, sem):
    flux_v[...] = result[PTS + 2 * OX:PTS + 2 * OX + AX, 0:AY]
    copies = [
        pltpu.make_async_copy(src, dst, sem.at[i])
        for i, (src, dst) in enumerate([
            (result.at[pl.ds(0, PTS)], atmos_out),
            (result.at[pl.ds(PTS, OX)], height_out),
            (result.at[pl.ds(PTS + OX, OX)], potential_out),
            (flux_v, flux_out),
        ])
    ]
    for copy in copies:
        copy.start()
    for copy in copies:
        copy.wait()


def on_device(
    atmos_state, wind_field, ocean_height, ocean_potential, ocean_neighbors, ocean_coupling,
    downward_source, downward_target, downward_weight,
    upward_source, upward_target, upward_weight,
):
    table = lambda value: value.reshape(NR, 128)
    any_spec = pl.BlockSpec(memory_space=pl.ANY)
    vm = lambda *shape, dtype=F32: pltpu.VMEM(shape, dtype)
    i32 = jnp.int32
    total_rows = PTS + 2 * OX + AX
    packed = pl.pallas_call(
        kernel,
        out_shape=pltpu.VMEM((total_rows, 128), F32),
        in_specs=[any_spec] * 13,
        out_specs=pl.BlockSpec(memory_space=pltpu.VMEM),
        scratch_shapes=[
            vm(PTS, 128), vm(2 * PTS, 128, dtype=jnp.bfloat16),
            vm(6, OX, OY, dtype=i32), vm(6, OX, OY),
            vm(NR, 128, dtype=i32), vm(NR, 128, dtype=i32), vm(NR, 128),
            vm(NR, 128, dtype=i32), vm(NR, 128, dtype=i32), vm(NR, 128),
            vm(3 * PTS, PTS),
            vm(3, 16, PTS), vm(2, NR, 128), vm(2, NR, 128), vm(2, 48, 128), vm(2, 56, 128),
            vm(8, ROWS, OY), vm(OX, OY), vm(ROWS, OY), vm(ROWS, OY),
            vm(2, ROWS, OY), vm(OX, OY), vm(ROWS, OY), vm(ROWS, OY),
            vm(8, 128), vm(2 * ROWS, 128), vm(OX, OY), vm(NR, 128),
            vm(2, NR, 128), vm(9, ROWS, 256),
            pltpu.SemaphoreType.DMA((13,)),
            pltpu.SemaphoreType.DMA((13,)), pltpu.SemaphoreType.DMA((12,)),
        ],
        compiler_params=pltpu.CompilerParams(
            collective_id=0, has_side_effects=True, vmem_limit_bytes=60 * 1024 * 1024
        ),
        name="coupled_step",
    )(
        atmos_state.reshape(PTS, 128), wind_field.reshape(2 * PTS, 128),
        ocean_height, ocean_potential, ocean_neighbors, ocean_coupling,
        table(downward_source), table(downward_target), table(downward_weight),
        table(upward_source), table(upward_target), table(upward_weight),
        jnp.asarray(point_operators()),
    )
    outs = pl.pallas_call(
        hand_out,
        out_shape=[
            jax.ShapeDtypeStruct((PTS, 128), F32),
            jax.ShapeDtypeStruct((OX, OY), F32),
            jax.ShapeDtypeStruct((OX, OY), F32),
            jax.ShapeDtypeStruct((AX, AY), F32),
        ],
        in_specs=[pl.BlockSpec(memory_space=pltpu.VMEM)],
        out_specs=[any_spec] * 4,
        scratch_shapes=[vm(AX, AY), pltpu.SemaphoreType.DMA((4,))],
        name="hand_out",
    )(pltpu.with_memory_space_constraint(packed, pltpu.VMEM))
    return (outs[0].reshape(AX, AY, 128), outs[1], outs[2], outs[3])


def solution(mesh):
    cells = P(None, "comp", "tile")
    tables = P("comp", "tile", None)
    flat = P("comp", "tile")
    return jax.shard_map(
        on_device,
        mesh=mesh,
        in_specs=(tables, P(None, "comp", "tile", None), flat, flat, cells, cells) + (tables,) * 6,
        out_specs=(tables, flat, flat, flat),
        check_vma=False,
    )
```

```python
import jax
import jax.numpy as jnp
import numpy as np
from jax import lax
from jax.experimental import pallas as pl
from jax.experimental.pallas import tpu as pltpu
from jax.sharding import PartitionSpec as P

F32 = jnp.float32
MESH = pl.DeviceIdType.MESH
HIGHEST = lax.Precision.HIGHEST
NT = (((1,), (1,)), ((), ()))
NN = (((1,), (0,)), ((), ()))

SUBSTEPS = 2
SUBCYCLES = 8
NC = 16
NR = 64
AX, AY = 8, 16
PTS = AX * AY
OX, OY = 32, 128
ROWS = OX + 16

atmos_step = 0.05
viscosity = 0.05
ocean_step = 0.2
wave_speed = 1.0
friction = 0.05

HALO, TABLE, EDGE, OCEAN, MATRIX, GATHER, UP, FAR = 0, 1, 2, 4, 7, 10, 11, 12


def gll_derivative():
    points = np.array([-1.0, -1.0 / np.sqrt(5.0), 1.0 / np.sqrt(5.0), 1.0])
    weights = np.array(
        [1.0 / np.prod([points[j] - points[k] for k in range(4) if k != j]) for j in range(4)]
    )
    matrix = np.zeros((4, 4))
    for i in range(4):
        for j in range(4):
            if i != j:
                matrix[i, j] = weights[j] / weights[i] / (points[i] - points[j])
        matrix[i, i] = -np.sum(matrix[i])
    return matrix


def point_operators():
    first = gll_derivative()
    second = first @ first
    along_x = lambda m: np.kron(np.kron(np.eye(AX // 4), m), np.eye(AY))
    along_y = lambda m: np.kron(np.eye(AX), np.kron(np.eye(AY // 4), m))
    curvature = viscosity * (along_x(second) + along_y(second))
    return np.concatenate([curvature, along_x(first), along_y(first)]).astype(np.float32)


def split_operators():
    whole = point_operators()
    high = whole.astype(jnp.bfloat16)
    rest = (whole - high.astype(np.float32)).astype(jnp.bfloat16)
    return np.concatenate([high, rest])


def iota(shape, dim):
    return lax.broadcasted_iota(jnp.int32, shape, dim)


def roll(x, shift, axis):
    return pltpu.roll(x, shift % x.shape[axis], axis)


def kernel(
    atmos_in, wind_in, height_in, potential_in, neigh_in, coup_in,
    dsrc_in, dtgt_in, dwgt_in, usrc_in, utgt_in, uwgt_in, oper_in,
    result,
    atmos_v, wind_v, neigh_v, coup_v, dsrc_v, dtgt_v, dwgt_v, usrc_v, utgt_v, uwgt_v, oper_v,
    surf_h, tab_s, tab_r, edge_s, edge_r, oc0, oc_pack, oc_right, oc_left,
    mx0, mx_pack, mx_right, mx_left, g_s, g_r, h_s, u_r, part_v, wst_v, pot_v,
    in_sem, ssem, rsem,
):
    c = lax.axis_index("comp")
    t = lax.axis_index("tile")
    k = t % 2
    r = t // 2
    z = t // 16
    y = (t // 2) % 8
    comp_at = lambda i: (c + i + NC) % NC
    comps = {i: comp_at(i) for i in (-1, 0, 1)}
    right = (t + 1) % NR
    left = (t + NR - 1) % NR
    own_q = k * 32 + r

    wrap = lambda value, size: jnp.where(value >= size, value - size, value)
    over_y = [wrap(y + i, 8) for i in (4, 5, 3, 6, 2, 7, 1, 0)]
    over_z = [8 * wrap(z + i, 4) for i in (2, 1, 3, 0)]
    chips = [zz + yy for yy in over_y for zz in over_z]
    row_order = [2 * chip + kk for chip in chips for kk in (1 - k, k)]
    peers = row_order[:-1]
    peer_chips = [chip for chip in chips for _ in range(2)][:-1]

    def at(dc, dt):
        row = comps[dc]
        col = t if dt == 0 else (right if dt > 0 else left)
        return (row, col)

    around = [(i, j) for i in (-1, 1, 0) for j in (-1, 1, 0) if (i, j) != (0, 0)]

    def send(src, dst, which, to, left_by=None):
        pltpu.make_async_remote_copy(
            src_ref=src, dst_ref=dst,
            send_sem=ssem.at[which if left_by is None else left_by], recv_sem=rsem.at[which],
            device_id=to, device_id_type=MESH,
        ).start()

    def take(ref, sem):
        pltpu.make_async_copy(ref, ref, sem).wait()

    barrier = pltpu.get_barrier_semaphore()

    def greet(to):
        pl.semaphore_signal(barrier, inc=1, device_id=to, device_id_type=MESH)


    for i in range(16):
        greet((comps[1], i))
        greet((comps[-1], 48 + i))
    for i, j in around:
        if i != 0:
            greet(at(i, j))
    loads = [
        pltpu.make_async_copy(src, dst, in_sem.at[i])
        for i, (src, dst) in enumerate([
            (atmos_in, atmos_v), (oper_in, oper_v), (wind_in, wind_v),
            (dsrc_in, dsrc_v), (usrc_in, usrc_v),
            (neigh_in, neigh_v), (coup_in, coup_v),
            (height_in, oc0.at[0, pl.ds(8, OX)]), (potential_in, oc0.at[1, pl.ds(8, OX)]),
            (dtgt_in, dtgt_v), (dwgt_in, dwgt_v), (utgt_in, utgt_v), (uwgt_in, uwgt_v),
        ])
    ]
    for load in loads:
        load.start()
    surf_h[:, 9:16, :] = jnp.zeros((3, 7, PTS), F32)


    for to in peers:
        greet((c, to))

    last = jnp.where(iota((16, 128), 1) == 127, 1.0, 0.0).astype(F32)
    loads[0].wait()
    loads[2].wait()
    atmos = atmos_v[...]
    surf_h[0, 4:5] = lax.dot_general(
        last[0:8], atmos, NT, precision=HIGHEST, preferred_element_type=F32
    )[0:1]
    winds = lax.dot_general(
        last.astype(jnp.bfloat16), wind_v[...], NT, preferred_element_type=F32
    )[0:1]
    surf_h[1, 4:5] = winds[:, 0:PTS]
    surf_h[2, 4:5] = winds[:, PTS:2 * PTS]
    east = wind_v[0:PTS].astype(F32)
    north = wind_v[PTS:2 * PTS].astype(F32)

    def parts(value):
        high = value.astype(jnp.bfloat16)
        return high, (value - high.astype(F32)).astype(jnp.bfloat16)

    def product(lhs, rhs, dims):
        return lax.dot_general(lhs, rhs, dims, preferred_element_type=F32)

    def rate_of(a):
        high, low = parts(a)
        both = product(oper_v[...], high, NN)
        res = both[0:3 * PTS] + (both[3 * PTS:6 * PTS] + product(oper_v[0:3 * PTS], low, NN))
        return res[0:PTS] - (east * res[PTS:2 * PTS] + north * res[2 * PTS:3 * PTS])

    def stage_edges(step, rate):
        edge_s[step, 0:16] = rate[0:16]
        edge_s[step, 16:32] = rate[112:128]
        shaped = rate.reshape(AX, AY, 128)
        edge_s[step, 32:40] = shaped[:, 0]
        edge_s[step, 40:48] = shaped[:, 15]

    def send_edges(step):
        s = lambda lo, n: edge_s.at[step, pl.ds(lo, n)]
        d = lambda lo, n: edge_r.at[step, pl.ds(lo, n)]
        which = EDGE + step
        send(s(0, 16), d(0, 16), which, at(-1, 0))
        send(s(16, 16), d(16, 16), which, at(1, 0))
        send(s(0, 1), d(48, 1), which, at(-1, -1))
        send(s(15, 1), d(49, 1), which, at(-1, 1))
        send(s(16, 1), d(50, 1), which, at(1, -1))
        send(s(31, 1), d(51, 1), which, at(1, 1))
        send(s(32, 8), d(32, 8), which, at(0, -1))
        send(s(40, 8), d(40, 8), which, at(0, 1))

    loads[3].wait()
    loads[4].wait()
    band = iota((NR, 128), 0)
    tab_s[0] = (dsrc_v[...] - 2 * band).astype(F32)
    tab_s[1] = (usrc_v[...] - 64 * band).astype(F32)
    for d in range(2):
        tab_r[d, pl.ds(own_q, 1)] = tab_s[d, pl.ds(t, 1)]

    far = jnp.where((z == 0) | (z == 3), 1, 0)
    pl.semaphore_wait(barrier, NR - 1 + 6 + NR * far)

    centre = pl.ds(4, 1)
    for i, j in around:
        send(surf_h.at[:, centre], surf_h.at[:, pl.ds(4 - 3 * i - j, 1)], HALO, at(i, j))

    for to in peers:
        send(tab_s.at[:, pl.ds(to, 1)], tab_r.at[:, pl.ds(own_q, 1)], TABLE, (c, to))
    loads[1].wait()
    rate0 = rate_of(atmos)
    stage_edges(0, rate0)

    send_edges(0)

    for i in (5, 6, 7, 8):
        loads[i].wait()
    base = iota((OX, OY), 0) * (OY + 2) + iota((OX, OY), 1)
    links = [(neigh_v[l] - base, coup_v[l]) for l in range(6)]

    def weight_of(di, dj):
        code = (di + 1) * (OY + 2) + dj + 1
        total = jnp.zeros((OX, OY), F32)
        for place, coef in links:
            total = total + jnp.where(place == code, coef, 0.0)
        return total

    own = slice(8, 8 + OX)
    oc0[2, own] = weight_of(-1, 0)
    oc0[3, own] = weight_of(1, 0)
    oc0[4, own] = weight_of(0, -1)
    oc0[5, own] = weight_of(0, 1)
    oc0[6, own] = weight_of(1, 1) - weight_of(1, -1)
    oc0[7, own] = weight_of(-1, -1) - weight_of(-1, 1)

    lane_o = iota((OX, OY), 1)

    def pack(fields):
        packed = jnp.zeros((OX, OY), F32)
        for f, value in enumerate(fields):
            packed = jnp.where(lane_o // 8 == f, roll(value, 8 * f, 1), packed)
            packed = jnp.where(lane_o // 8 == 8 + f, roll(value, 72 + 8 * f, 1), packed)
        return packed

    def send_block(full, packed, rt, lf, which):
        top, bottom = pl.ds(0, 8), pl.ds(24, 8)
        above, below, beside = pl.ds(0, 8), pl.ds(8 + OX, 8), pl.ds(8, OX)
        send(full.at[:, pl.ds(OX, 8)], full.at[:, above], which, at(1, 0))
        send(full.at[:, pl.ds(8, 8)], full.at[:, below], which, at(-1, 0))
        send(packed.at[bottom], rt.at[above], which + 1, at(1, -1))
        send(packed.at[top], rt.at[below], which + 1, at(-1, -1))
        send(packed, rt.at[beside], which + 1, at(0, -1))
        send(packed.at[bottom], lf.at[above], which + 2, at(1, 1))
        send(packed.at[top], lf.at[below], which + 2, at(-1, 1))
        send(packed, lf.at[beside], which + 2, at(0, 1))

    def take_block(full, rt, lf, sems, which):
        take(full.at[:, pl.ds(0, 16)], sems.at[which])
        take(rt, sems.at[which + 1])
        take(lf, sems.at[which + 2])

    lane_x = iota((ROWS, OY), 1)

    def beside(rt, lf, f):
        from_right = roll(rt, -8 * f, 1)
        from_left = roll(lf, 56 - 8 * f, 1)
        return jnp.where(lane_x < 8, from_right, jnp.where(lane_x >= 120, from_left, 0.0))

    oc_pack[...] = pack([oc0[f, own] for f in range(8)])

    send_block(oc0, oc_pack, oc_right, oc_left, OCEAN)

    lane_s = iota((16, PTS), 1)
    xs, ys = lane_s // AY, lane_s % AY

    def pairs(values, after, before, pos):
        return jnp.where(
            pos == 3, 0.5 * (values + after), jnp.where(pos == 0, 0.5 * (values + before), values)
        )

    take(edge_r.at[0, pl.ds(0, 24)], rsem.at[HALO])
    surf = surf_h[0]
    surf_e = surf_h[1]
    surf_n = surf_h[2]
    for _ in range(SUBSTEPS):
        high, low = parts(surf)
        both = product(jnp.concatenate([high, low], axis=0), oper_v[0:3 * PTS], NT)
        res = both[0:16] + (both[16:32] + product(high, oper_v[3 * PTS:6 * PTS], NT))
        rate = res[:, 0:PTS] - (surf_e * res[:, PTS:2 * PTS] + surf_n * res[:, 2 * PTS:3 * PTS])
        nxt, prv = roll(rate, -16, 1), roll(rate, 16, 1)
        after = jnp.where(xs == AX - 1, roll(nxt, -3, 0), nxt)
        before = jnp.where(xs == 0, roll(prv, 3, 0), prv)
        rate = pairs(rate, after, before, xs % 4)
        after = jnp.where(ys == AY - 1, roll(roll(rate, 15, 1), -1, 0), roll(rate, -1, 1))
        before = jnp.where(ys == 0, roll(roll(rate, -15, 1), 1, 0), roll(rate, 1, 1))
        surf = surf + atmos_step * pairs(rate, after, before, ys % 4)
    g_s[0:1] = surf[4:5]
    mine = pl.ds(k * ROWS + 8 + r, 1)
    g_r[mine] = g_s[0:1]

    @pl.when(far == 1)
    def _():
        row = jnp.where(z == 0, comps[-1], comps[1])
        place = pl.ds(k * ROWS + jnp.where(z == 0, 8 + OX, 0) + y, 1)
        for to in row_order:
            send(g_s.at[pl.ds(0, 1)], g_r.at[place], GATHER, (row, to), FAR)

    for to in peers:
        send(g_s.at[pl.ds(0, 1)], g_r.at[mine], GATHER, (c, to))

    row_q = iota((NR, 128), 0)
    peer_q = 2 * (row_q % 32) + row_q // 32
    lane_64 = iota((NR, 128), 1)

    def by_core(ref):
        return jnp.concatenate(
            [ref[pl.ds(0, 32, stride=2), :], ref[pl.ds(1, 32, stride=2), :]], axis=0
        )

    def turned(value):
        tall = jnp.concatenate([value, jnp.zeros((128 - NR, 128), F32)], axis=0).T
        return jnp.where(lane_64 < 64, tall[0:64], roll(tall[64:128], 64, 1))

    def matrices(cell, second, weight):
        cell_t = turned(cell)
        one = weight * second
        one_t = turned(one)
        zero_t = turned(weight - one)

        def group(g, carry):
            for i in range(8):
                n = g * 8 + i
                hit = cell_t == n.astype(F32)
                part_v[0, pl.ds(n, 1)] = jnp.sum(jnp.where(hit, zero_t, 0.0), axis=0, keepdims=True)
                part_v[1, pl.ds(n, 1)] = jnp.sum(jnp.where(hit, one_t, 0.0), axis=0, keepdims=True)
            return carry

        lax.fori_loop(0, 8, group, 0)
        return [part_v[j] + roll(part_v[j], 64, 1) for j in range(2)]

    for i in (9, 10):
        loads[i].wait()
    take(tab_r.at[:, pl.ds(0, NR - 1)], rsem.at[TABLE])
    down = matrices(
        (by_core(dtgt_v) - 64 * peer_q).astype(F32), tab_r[0], by_core(dwgt_v)
    )
    for j in range(2):
        cells = jnp.concatenate([down[j], roll(down[j], -32, 1)], axis=0).T
        mx0[j, own] = cells[0:OX]
    mx_pack[...] = pack([mx0[j, own] for j in range(2)])
    send_block(mx0, mx_pack, mx_right, mx_left, MATRIX)

    row_a = iota((PTS, 128), 0)
    xa, ya = row_a // AY, row_a % AY
    row_e = iota((AX, 128), 0)

    def finish(step, a, rate):
        take(edge_r.at[step, pl.ds(0, 52)], rsem.at[EDGE + step])
        recv = lambda lo, n: edge_r[step, lo:lo + n]
        after = jnp.concatenate([rate[16:128], recv(0, 16)], axis=0)
        before = jnp.concatenate([recv(16, 16), rate[0:112]], axis=0)
        across = pairs(rate, after, before, xa % 4)

        def column(lo, beyond, ahead):
            col = recv(lo, 8)
            nxt = jnp.where(row_e == 7, beyond, roll(col, -1, 0))
            prv = jnp.where(row_e == 0, ahead, roll(col, 1, 0))
            col = pairs(col, nxt, prv, row_e % 4)
            return jnp.broadcast_to(col[:, None, :], (AX, AY, 128)).reshape(PTS, 128)

        east_col = column(32, recv(48, 1), recv(50, 1))
        west_col = column(40, recv(49, 1), recv(51, 1))
        after = jnp.where(ya == AY - 1, east_col, roll(across, -1, 0))
        before = jnp.where(ya == 0, west_col, roll(across, 1, 0))
        return a + atmos_step * pairs(across, after, before, ya % 4)

    atmos = finish(0, atmos, rate0)
    rate1 = rate_of(atmos)
    stage_edges(1, rate1)
    send_edges(1)

    take_block(oc0, oc_right, oc_left, rsem, OCEAN)
    oc_rt, oc_lf = oc_right[...], oc_left[...]
    wide = [(oc0[f], beside(oc_rt, oc_lf, f)) for f in range(8)]

    def shifted(pair, step):
        a, b = (roll(v, step, 1) for v in pair)
        edge = lane_x == (0 if step == 1 else OY - 1)
        return jnp.where(edge, b, a), jnp.where(edge, a, b)

    height, potential = list(wide[0]), list(wide[1])
    w_n, w_s, w_w, w_e, pair_s, pair_n = [
        tuple(ocean_step * v for v in pair) for pair in wide[2:]
    ]
    positive = lambda pair: tuple(jnp.maximum(v, 0.0) for v in pair)
    negative = lambda pair: tuple(jnp.maximum(-v, 0.0) for v in pair)
    w_se, w_sw = positive(pair_s), negative(pair_s)
    w_nw, w_ne = positive(pair_n), negative(pair_n)
    w_c = tuple(
        -(n + s + w + e + abs(ps) + abs(pn))
        for n, s, w, e, ps, pn in zip(w_n, w_s, w_w, w_e, pair_s, pair_n)
    )
    for i, (value, shift) in enumerate([
        (w_nw, -1), (w_w, -1), (w_sw, -1),
        (w_n, 0), (w_c, 0), (w_s, 0),
        (w_ne, 1), (w_e, 1), (w_se, 1),
    ]):
        value = value if shift == 0 else shifted(value, shift)
        for half in range(2):
            wst_v[i, half] = value[half]
    for half in range(2):
        pot_v[half, 0:8] = jnp.zeros((8, OY), F32)
        pot_v[half, 8 + ROWS:16 + ROWS] = jnp.zeros((8, OY), F32)

    take_block(mx0, mx_right, mx_left, rsem, MATRIX)
    mx_rt, mx_lf = mx_right[...], mx_left[...]
    mx1 = [beside(mx_rt, mx_lf, j) for j in range(2)]
    take(g_r.at[pl.ds(0, 95)], rsem.at[GATHER])
    even, odd = g_r[0:ROWS], g_r[ROWS:2 * ROWS]

    def column_of(block, point):
        return jnp.sum(jnp.where(lane_x == point, block, 0.0), axis=1, keepdims=True)

    near = jnp.zeros((ROWS, OY), F32)
    side = jnp.zeros((ROWS, OY), F32)
    for j in range(2):
        here = jnp.where(lane_x < 64, column_of(even, 2 * t + j), column_of(odd, 2 * t + j))
        there = jnp.where(
            lane_x < 64, column_of(even, 2 * right + j), column_of(odd, 2 * left + j)
        )
        near = near + mx0[j] * here
        side = side + mx1[j] * there
    forcing = (ocean_step * near, ocean_step * side)

    for _ in range(SUBCYCLES):
        for half in range(2):
            potential[half] = (
                (1.0 - friction) * potential[half]
                + ((ocean_step * wave_speed) * height[half] + forcing[half])
            )
            pot_v[half, 8:8 + ROWS] = potential[half]
        sums = [[], [], []]
        for half in range(2):
            above = pot_v[half, 7:7 + ROWS]
            below = pot_v[half, 9:9 + ROWS]
            for j in range(3):
                sums[j].append(
                    wst_v[3 * j, half] * above
                    + wst_v[3 * j + 1, half] * potential[half]
                    + wst_v[3 * j + 2, half] * below
                )
        west, east_sum = shifted(sums[0], 1), shifted(sums[2], -1)
        for half in range(2):
            height[half] = (height[half] + sums[1][half]) + (west[half] + east_sum[half])

    h_s[...] = height[0][own]
    u_r[pl.ds(own_q, 1)] = h_s[pl.ds(r, 1)]
    for to, chip in zip(peers, peer_chips):
        send(h_s.at[pl.ds(chip, 1)], u_r.at[pl.ds(own_q, 1)], UP, (c, to))
    result[PTS:PTS + OX] = height[0][own]
    result[PTS + OX:PTS + 2 * OX] = potential[0][own]

    atmos = finish(1, atmos, rate1)
    result[0:PTS] = atmos

    for i in (11, 12):
        loads[i].wait()
    upward = matrices(
        tab_r[1], (by_core(utgt_v) - 2 * peer_q).astype(F32), by_core(uwgt_v)
    )
    up_cells = []
    blank = jnp.zeros((NR, 128), F32)
    for j in range(2):
        low = jnp.where(k == 0, upward[j], blank)
        high = jnp.where(k == 0, blank, upward[j])
        up_cells.append(jnp.concatenate([low, high], axis=0).T[0:NR])

    take(edge_r.at[0, pl.ds(0, 24)], ssem.at[HALO])
    take(tab_r.at[:, pl.ds(0, NR - 1)], ssem.at[TABLE])
    take(edge_r.at[0, pl.ds(0, 52)], ssem.at[EDGE])
    take(edge_r.at[1, pl.ds(0, 52)], ssem.at[EDGE + 1])
    take_block(oc0, oc_right, oc_left, ssem, OCEAN)
    take_block(mx0, mx_right, mx_left, ssem, MATRIX)
    take(g_r.at[pl.ds(0, NR - 1)], ssem.at[GATHER])

    @pl.when(far == 1)
    def _():
        take(g_r.at[pl.ds(0, NR)], ssem.at[FAR])

    q_row = iota((AX, NR), 1)
    pick = jnp.where((q_row % 32) // 4 == iota((AX, NR), 0), 1.0, 0.0).astype(F32)
    column0 = 4 * (row_q % 4) + 2 * (row_q // 32)
    take(u_r.at[pl.ds(0, NR - 1)], rsem.at[UP])
    cells = u_r[...]
    spread = jnp.zeros((NR, 128), F32)
    for j in range(2):
        total = jnp.sum(up_cells[j] * cells, axis=1, keepdims=True)
        spread = spread + jnp.where(lane_64 == column0 + j, total, 0.0)
    flux = lax.dot_general(pick, spread, NN, precision=HIGHEST, preferred_element_type=F32)
    result[PTS + 2 * OX:PTS + 2 * OX + AX] = flux
    take(u_r.at[pl.ds(0, NR - 1)], ssem.at[UP])


def hand_out(result, atmos_out, height_out, potential_out, flux_out, flux_v, sem):
    flux_v[...] = result[PTS + 2 * OX:PTS + 2 * OX + AX, 0:AY]
    copies = [
        pltpu.make_async_copy(src, dst, sem.at[i])
        for i, (src, dst) in enumerate([
            (result.at[pl.ds(0, PTS)], atmos_out),
            (result.at[pl.ds(PTS, OX)], height_out),
            (result.at[pl.ds(PTS + OX, OX)], potential_out),
            (flux_v, flux_out),
        ])
    ]
    for copy in copies:
        copy.start()
    for copy in copies:
        copy.wait()


def on_device(
    atmos_state, wind_field, ocean_height, ocean_potential, ocean_neighbors, ocean_coupling,
    downward_source, downward_target, downward_weight,
    upward_source, upward_target, upward_weight,
):
    table = lambda value: value.reshape(NR, 128)
    any_spec = pl.BlockSpec(memory_space=pl.ANY)
    vm = lambda *shape, dtype=F32: pltpu.VMEM(shape, dtype)
    i32 = jnp.int32
    total_rows = PTS + 2 * OX + AX
    packed = pl.pallas_call(
        kernel,
        out_shape=pltpu.VMEM((total_rows, 128), F32),
        in_specs=[any_spec] * 13,
        out_specs=pl.BlockSpec(memory_space=pltpu.VMEM),
        scratch_shapes=[
            vm(PTS, 128), vm(2 * PTS, 128, dtype=jnp.bfloat16),
            vm(6, OX, OY, dtype=i32), vm(6, OX, OY),
            vm(NR, 128, dtype=i32), vm(NR, 128, dtype=i32), vm(NR, 128),
            vm(NR, 128, dtype=i32), vm(NR, 128, dtype=i32), vm(NR, 128),
            vm(6 * PTS, PTS, dtype=jnp.bfloat16),
            vm(3, 16, PTS), vm(2, NR, 128), vm(2, NR, 128), vm(2, 48, 128), vm(2, 56, 128),
            vm(8, ROWS, OY), vm(OX, OY), vm(ROWS, OY), vm(ROWS, OY),
            vm(2, ROWS, OY), vm(OX, OY), vm(ROWS, OY), vm(ROWS, OY),
            vm(8, 128), vm(2 * ROWS, 128), vm(OX, OY), vm(NR, 128),
            vm(2, NR, 128), vm(9, 2, ROWS, OY), vm(2, ROWS + 16, OY),
            pltpu.SemaphoreType.DMA((13,)),
            pltpu.SemaphoreType.DMA((13,)), pltpu.SemaphoreType.DMA((12,)),
        ],
        compiler_params=pltpu.CompilerParams(
            collective_id=0, has_side_effects=True, vmem_limit_bytes=60 * 1024 * 1024
        ),
        name="coupled_step",
    )(
        atmos_state.reshape(PTS, 128), wind_field.reshape(2 * PTS, 128),
        ocean_height, ocean_potential, ocean_neighbors, ocean_coupling,
        table(downward_source), table(downward_target), table(downward_weight),
        table(upward_source), table(upward_target), table(upward_weight),
        jnp.asarray(split_operators()),
    )
    outs = pl.pallas_call(
        hand_out,
        out_shape=[
            jax.ShapeDtypeStruct((PTS, 128), F32),
            jax.ShapeDtypeStruct((OX, OY), F32),
            jax.ShapeDtypeStruct((OX, OY), F32),
            jax.ShapeDtypeStruct((AX, AY), F32),
        ],
        in_specs=[pl.BlockSpec(memory_space=pltpu.VMEM)],
        out_specs=[any_spec] * 4,
        scratch_shapes=[vm(AX, AY), pltpu.SemaphoreType.DMA((4,))],
        name="hand_out",
    )(pltpu.with_memory_space_constraint(packed, pltpu.VMEM))
    return (outs[0].reshape(AX, AY, 128), outs[1], outs[2], outs[3])


def solution(mesh):
    cells = P(None, "comp", "tile")
    tables = P("comp", "tile", None)
    flat = P("comp", "tile")
    return jax.shard_map(
        on_device,
        mesh=mesh,
        in_specs=(tables, P(None, "comp", "tile", None), flat, flat, cells, cells) + (tables,) * 6,
        out_specs=(tables, flat, flat, flat),
        check_vma=False,
    )
```

```python
import jax
import jax.numpy as jnp
import numpy as np
from jax import lax
from jax.experimental import pallas as pl
from jax.experimental.pallas import tpu as pltpu
from jax.sharding import PartitionSpec as P

F32 = jnp.float32
MESH = pl.DeviceIdType.MESH
HIGHEST = lax.Precision.HIGHEST
NT = (((1,), (1,)), ((), ()))
NN = (((1,), (0,)), ((), ()))

SUBSTEPS = 2
SUBCYCLES = 8
NC = 16
NR = 64
AX, AY = 8, 16
PTS = AX * AY
OX, OY = 32, 128
ROWS = OX + 16

atmos_step = 0.05
viscosity = 0.05
ocean_step = 0.2
wave_speed = 1.0
friction = 0.05

HALO, TABLE, EDGE, OCEAN, MATRIX, GATHER, UP, TABLE_UP, FAR = 0, 1, 2, 4, 7, 10, 11, 12, 13


def gll_derivative():
    points = np.array([-1.0, -1.0 / np.sqrt(5.0), 1.0 / np.sqrt(5.0), 1.0])
    weights = np.array(
        [1.0 / np.prod([points[j] - points[k] for k in range(4) if k != j]) for j in range(4)]
    )
    matrix = np.zeros((4, 4))
    for i in range(4):
        for j in range(4):
            if i != j:
                matrix[i, j] = weights[j] / weights[i] / (points[i] - points[j])
        matrix[i, i] = -np.sum(matrix[i])
    return matrix


def point_operators():
    first = gll_derivative()
    second = first @ first
    along_x = lambda m: np.kron(np.kron(np.eye(AX // 4), m), np.eye(AY))
    along_y = lambda m: np.kron(np.eye(AX), np.kron(np.eye(AY // 4), m))
    curvature = viscosity * (along_x(second) + along_y(second))
    return np.concatenate([curvature, along_x(first), along_y(first)]).astype(np.float32)


def split_operators():
    whole = point_operators()
    high = whole.astype(jnp.bfloat16)
    rest = (whole - high.astype(np.float32)).astype(jnp.bfloat16)
    return np.concatenate([high, rest])


def iota(shape, dim):
    return lax.broadcasted_iota(jnp.int32, shape, dim)


def roll(x, shift, axis):
    return pltpu.roll(x, shift % x.shape[axis], axis)


def kernel(
    atmos_in, wind_in, height_in, potential_in, neigh_in, coup_in,
    dsrc_in, dtgt_in, dwgt_in, usrc_in, utgt_in, uwgt_in, oper_in,
    result,
    atmos_v, wind_v, neigh_v, coup_v, dsrc_v, dtgt_v, dwgt_v, usrc_v, utgt_v, uwgt_v, oper_v,
    surf_h, tab_s, tab_r, edge_s, edge_r, oc0, oc_pack, oc_right, oc_left,
    mx0, mx_pack, mx_right, mx_left, g_s, g_r, h_s, u_r, part_v, wst_v, pot_v,
    in_sem, ssem, rsem,
):
    c = lax.axis_index("comp")
    t = lax.axis_index("tile")
    k = t % 2
    r = t // 2
    z = t // 16
    y = (t // 2) % 8
    comp_at = lambda i: (c + i + NC) % NC
    comps = {i: comp_at(i) for i in (-1, 0, 1)}
    right = (t + 1) % NR
    left = (t + NR - 1) % NR
    own_q = k * 32 + r

    wrap = lambda value, size: jnp.where(value >= size, value - size, value)
    over_y = [wrap(y + i, 8) for i in (4, 5, 3, 6, 2, 7, 1, 0)]
    over_z = [8 * wrap(z + i, 4) for i in (2, 1, 3, 0)]
    chips = [zz + yy for yy in over_y for zz in over_z]
    row_order = [2 * chip + kk for chip in chips for kk in (1 - k, k)]
    peers = row_order[:-1]
    peer_chips = [chip for chip in chips for _ in range(2)][:-1]

    def at(dc, dt):
        row = comps[dc]
        col = t if dt == 0 else (right if dt > 0 else left)
        return (row, col)

    around = [(i, j) for i in (-1, 1, 0) for j in (-1, 1, 0) if (i, j) != (0, 0)]

    def send(src, dst, which, to, left_by=None):
        pltpu.make_async_remote_copy(
            src_ref=src, dst_ref=dst,
            send_sem=ssem.at[which if left_by is None else left_by], recv_sem=rsem.at[which],
            device_id=to, device_id_type=MESH,
        ).start()

    def take(ref, sem):
        pltpu.make_async_copy(ref, ref, sem).wait()

    barrier = pltpu.get_barrier_semaphore()

    def greet(to):
        pl.semaphore_signal(barrier, inc=1, device_id=to, device_id_type=MESH)


    for i in range(16):
        greet((comps[1], i))
        greet((comps[-1], 48 + i))
    for i, j in around:
        if i != 0:
            greet(at(i, j))
    loads = [
        pltpu.make_async_copy(src, dst, in_sem.at[i])
        for i, (src, dst) in enumerate([
            (atmos_in, atmos_v), (oper_in, oper_v), (wind_in, wind_v),
            (dsrc_in, dsrc_v), (usrc_in, usrc_v),
            (neigh_in, neigh_v), (coup_in, coup_v),
            (height_in, oc0.at[0, pl.ds(8, OX)]), (potential_in, oc0.at[1, pl.ds(8, OX)]),
            (dtgt_in, dtgt_v), (dwgt_in, dwgt_v), (utgt_in, utgt_v), (uwgt_in, uwgt_v),
        ])
    ]
    for load in loads:
        load.start()
    surf_h[:, 9:16, :] = jnp.zeros((3, 7, PTS), F32)


    for to in peers:
        greet((c, to))

    last = jnp.where(iota((16, 128), 1) == 127, 1.0, 0.0).astype(F32)
    loads[0].wait()
    loads[2].wait()
    atmos = atmos_v[...]
    surf_h[0, 4:5] = lax.dot_general(
        last[0:8], atmos, NT, precision=HIGHEST, preferred_element_type=F32
    )[0:1]
    winds = lax.dot_general(
        last.astype(jnp.bfloat16), wind_v[...], NT, preferred_element_type=F32
    )[0:1]
    surf_h[1, 4:5] = winds[:, 0:PTS]
    surf_h[2, 4:5] = winds[:, PTS:2 * PTS]
    east = wind_v[0:PTS].astype(F32)
    north = wind_v[PTS:2 * PTS].astype(F32)

    def parts(value):
        high = value.astype(jnp.bfloat16)
        return high, (value - high.astype(F32)).astype(jnp.bfloat16)

    def product(lhs, rhs, dims):
        return lax.dot_general(lhs, rhs, dims, preferred_element_type=F32)

    def rate_of(a):
        high, low = parts(a)
        both = product(oper_v[...], high, NN)
        res = both[0:3 * PTS] + (both[3 * PTS:6 * PTS] + product(oper_v[0:3 * PTS], low, NN))
        return res[0:PTS] - (east * res[PTS:2 * PTS] + north * res[2 * PTS:3 * PTS])

    def stage_edges(step, rate):
        edge_s[step, 0:16] = rate[0:16]
        edge_s[step, 16:32] = rate[112:128]
        shaped = rate.reshape(AX, AY, 128)
        edge_s[step, 32:40] = shaped[:, 0]
        edge_s[step, 40:48] = shaped[:, 15]

    def send_edges(step):
        s = lambda lo, n: edge_s.at[step, pl.ds(lo, n)]
        d = lambda lo, n: edge_r.at[step, pl.ds(lo, n)]
        which = EDGE + step
        send(s(0, 16), d(0, 16), which, at(-1, 0))
        send(s(16, 16), d(16, 16), which, at(1, 0))
        send(s(0, 1), d(48, 1), which, at(-1, -1))
        send(s(15, 1), d(49, 1), which, at(-1, 1))
        send(s(16, 1), d(50, 1), which, at(1, -1))
        send(s(31, 1), d(51, 1), which, at(1, 1))
        send(s(32, 8), d(32, 8), which, at(0, -1))
        send(s(40, 8), d(40, 8), which, at(0, 1))

    loads[3].wait()
    loads[4].wait()
    band = iota((NR, 128), 0)
    tab_s[0] = (dsrc_v[...] - 2 * band).astype(F32)
    tab_s[1] = (usrc_v[...] - 64 * band).astype(F32)
    for d in range(2):
        tab_r[d, pl.ds(own_q, 1)] = tab_s[d, pl.ds(t, 1)]

    far = jnp.where((z == 0) | (z == 3), 1, 0)
    pl.semaphore_wait(barrier, NR - 1 + 6 + NR * far)

    centre = pl.ds(4, 1)
    for i, j in around:
        send(surf_h.at[:, centre], surf_h.at[:, pl.ds(4 - 3 * i - j, 1)], HALO, at(i, j))

    for to in peers:
        send(tab_s.at[0, pl.ds(to, 1)], tab_r.at[0, pl.ds(own_q, 1)], TABLE, (c, to))
    loads[1].wait()
    rate0 = rate_of(atmos)
    stage_edges(0, rate0)

    send_edges(0)

    for i in (5, 6, 7, 8):
        loads[i].wait()
    base = iota((OX, OY), 0) * (OY + 2) + iota((OX, OY), 1)
    links = [(neigh_v[l] - base, coup_v[l]) for l in range(6)]

    def weight_of(di, dj):
        code = (di + 1) * (OY + 2) + dj + 1
        total = jnp.zeros((OX, OY), F32)
        for place, coef in links:
            total = total + jnp.where(place == code, coef, 0.0)
        return total

    own = slice(8, 8 + OX)
    oc0[2, own] = weight_of(-1, 0)
    oc0[3, own] = weight_of(1, 0)
    oc0[4, own] = weight_of(0, -1)
    oc0[5, own] = weight_of(0, 1)
    oc0[6, own] = weight_of(1, 1) - weight_of(1, -1)
    oc0[7, own] = weight_of(-1, -1) - weight_of(-1, 1)

    lane_o = iota((OX, OY), 1)

    def pack(fields):
        packed = jnp.zeros((OX, OY), F32)
        for f, value in enumerate(fields):
            packed = jnp.where(lane_o // 8 == f, roll(value, 8 * f, 1), packed)
            packed = jnp.where(lane_o // 8 == 8 + f, roll(value, 72 + 8 * f, 1), packed)
        return packed

    def send_block(full, packed, rt, lf, which):
        top, bottom = pl.ds(0, 8), pl.ds(24, 8)
        above, below, beside = pl.ds(0, 8), pl.ds(8 + OX, 8), pl.ds(8, OX)
        send(full.at[:, pl.ds(OX, 8)], full.at[:, above], which, at(1, 0))
        send(full.at[:, pl.ds(8, 8)], full.at[:, below], which, at(-1, 0))
        send(packed.at[bottom], rt.at[above], which + 1, at(1, -1))
        send(packed.at[top], rt.at[below], which + 1, at(-1, -1))
        send(packed, rt.at[beside], which + 1, at(0, -1))
        send(packed.at[bottom], lf.at[above], which + 2, at(1, 1))
        send(packed.at[top], lf.at[below], which + 2, at(-1, 1))
        send(packed, lf.at[beside], which + 2, at(0, 1))

    def take_block(full, rt, lf, sems, which):
        take(full.at[:, pl.ds(0, 16)], sems.at[which])
        take(rt, sems.at[which + 1])
        take(lf, sems.at[which + 2])

    lane_x = iota((ROWS, OY), 1)

    def beside(rt, lf, f):
        from_right = roll(rt, -8 * f, 1)
        from_left = roll(lf, 56 - 8 * f, 1)
        return jnp.where(lane_x < 8, from_right, jnp.where(lane_x >= 120, from_left, 0.0))

    oc_pack[...] = pack([oc0[f, own] for f in range(8)])

    send_block(oc0, oc_pack, oc_right, oc_left, OCEAN)

    lane_s = iota((16, PTS), 1)
    xs, ys = lane_s // AY, lane_s % AY

    def pairs(values, after, before, pos):
        return jnp.where(
            pos == 3, 0.5 * (values + after), jnp.where(pos == 0, 0.5 * (values + before), values)
        )

    take(edge_r.at[0, pl.ds(0, 24)], rsem.at[HALO])
    surf = surf_h[0]
    surf_e = surf_h[1]
    surf_n = surf_h[2]
    for _ in range(SUBSTEPS):
        high, low = parts(surf)
        both = product(jnp.concatenate([high, low], axis=0), oper_v[0:3 * PTS], NT)
        res = both[0:16] + (both[16:32] + product(high, oper_v[3 * PTS:6 * PTS], NT))
        rate = res[:, 0:PTS] - (surf_e * res[:, PTS:2 * PTS] + surf_n * res[:, 2 * PTS:3 * PTS])
        nxt, prv = roll(rate, -16, 1), roll(rate, 16, 1)
        after = jnp.where(xs == AX - 1, roll(nxt, -3, 0), nxt)
        before = jnp.where(xs == 0, roll(prv, 3, 0), prv)
        rate = pairs(rate, after, before, xs % 4)
        after = jnp.where(ys == AY - 1, roll(roll(rate, 15, 1), -1, 0), roll(rate, -1, 1))
        before = jnp.where(ys == 0, roll(roll(rate, -15, 1), 1, 0), roll(rate, 1, 1))
        surf = surf + atmos_step * pairs(rate, after, before, ys % 4)
    g_s[0:1] = surf[4:5]
    mine = pl.ds(k * ROWS + 8 + r, 1)
    g_r[mine] = g_s[0:1]

    @pl.when(far == 1)
    def _():
        row = jnp.where(z == 0, comps[-1], comps[1])
        place = pl.ds(k * ROWS + jnp.where(z == 0, 8 + OX, 0) + y, 1)
        for to in row_order:
            send(g_s.at[pl.ds(0, 1)], g_r.at[place], GATHER, (row, to), FAR)

    for to in peers:
        send(g_s.at[pl.ds(0, 1)], g_r.at[mine], GATHER, (c, to))

    row_q = iota((NR, 128), 0)
    peer_q = 2 * (row_q % 32) + row_q // 32
    lane_64 = iota((NR, 128), 1)

    def by_core(ref):
        return jnp.concatenate(
            [ref[pl.ds(0, 32, stride=2), :], ref[pl.ds(1, 32, stride=2), :]], axis=0
        )

    def turned(value):
        tall = jnp.concatenate([value, jnp.zeros((128 - NR, 128), F32)], axis=0).T
        return jnp.where(lane_64 < 64, tall[0:64], roll(tall[64:128], 64, 1))

    def matrices(cell, second, weight):
        cell_t = turned(cell)
        one = weight * second
        one_t = turned(one)
        zero_t = turned(weight - one)

        def group(g, carry):
            for i in range(8):
                n = g * 8 + i
                hit = cell_t == n.astype(F32)
                part_v[0, pl.ds(n, 1)] = jnp.sum(jnp.where(hit, zero_t, 0.0), axis=0, keepdims=True)
                part_v[1, pl.ds(n, 1)] = jnp.sum(jnp.where(hit, one_t, 0.0), axis=0, keepdims=True)
            return carry

        lax.fori_loop(0, 8, group, 0)
        return [part_v[j] + roll(part_v[j], 64, 1) for j in range(2)]

    for i in (9, 10):
        loads[i].wait()
    take(tab_r.at[0, pl.ds(0, NR - 1)], rsem.at[TABLE])
    down = matrices(
        (by_core(dtgt_v) - 64 * peer_q).astype(F32), tab_r[0], by_core(dwgt_v)
    )
    for j in range(2):
        cells = jnp.concatenate([down[j], roll(down[j], -32, 1)], axis=0).T
        mx0[j, own] = cells[0:OX]
    mx_pack[...] = pack([mx0[j, own] for j in range(2)])
    send_block(mx0, mx_pack, mx_right, mx_left, MATRIX)

    row_a = iota((PTS, 128), 0)
    xa, ya = row_a // AY, row_a % AY
    row_e = iota((AX, 128), 0)

    def finish(step, a, rate):
        take(edge_r.at[step, pl.ds(0, 52)], rsem.at[EDGE + step])
        recv = lambda lo, n: edge_r[step, lo:lo + n]
        after = jnp.concatenate([rate[16:128], recv(0, 16)], axis=0)
        before = jnp.concatenate([recv(16, 16), rate[0:112]], axis=0)
        across = pairs(rate, after, before, xa % 4)

        def column(lo, beyond, ahead):
            col = recv(lo, 8)
            nxt = jnp.where(row_e == 7, beyond, roll(col, -1, 0))
            prv = jnp.where(row_e == 0, ahead, roll(col, 1, 0))
            col = pairs(col, nxt, prv, row_e % 4)
            return jnp.broadcast_to(col[:, None, :], (AX, AY, 128)).reshape(PTS, 128)

        east_col = column(32, recv(48, 1), recv(50, 1))
        west_col = column(40, recv(49, 1), recv(51, 1))
        after = jnp.where(ya == AY - 1, east_col, roll(across, -1, 0))
        before = jnp.where(ya == 0, west_col, roll(across, 1, 0))
        return a + atmos_step * pairs(across, after, before, ya % 4)

    for to in peers:
        send(tab_s.at[1, pl.ds(to, 1)], tab_r.at[1, pl.ds(own_q, 1)], TABLE_UP, (c, to))
    atmos = finish(0, atmos, rate0)
    rate1 = rate_of(atmos)
    stage_edges(1, rate1)
    send_edges(1)

    take_block(oc0, oc_right, oc_left, rsem, OCEAN)
    oc_rt, oc_lf = oc_right[...], oc_left[...]
    wide = [(oc0[f], beside(oc_rt, oc_lf, f)) for f in range(8)]

    def shifted(pair, step):
        a, b = (roll(v, step, 1) for v in pair)
        edge = lane_x == (0 if step == 1 else OY - 1)
        return jnp.where(edge, b, a), jnp.where(edge, a, b)

    height, potential = list(wide[0]), list(wide[1])
    w_n, w_s, w_w, w_e, pair_s, pair_n = [
        tuple(ocean_step * v for v in pair) for pair in wide[2:]
    ]
    positive = lambda pair: tuple(jnp.maximum(v, 0.0) for v in pair)
    negative = lambda pair: tuple(jnp.maximum(-v, 0.0) for v in pair)
    w_se, w_sw = positive(pair_s), negative(pair_s)
    w_nw, w_ne = positive(pair_n), negative(pair_n)
    w_c = tuple(
        -(n + s + w + e + abs(ps) + abs(pn))
        for n, s, w, e, ps, pn in zip(w_n, w_s, w_w, w_e, pair_s, pair_n)
    )
    for i, (value, shift) in enumerate([
        (w_nw, -1), (w_w, -1), (w_sw, -1),
        (w_n, 0), (w_c, 0), (w_s, 0),
        (w_ne, 1), (w_e, 1), (w_se, 1),
    ]):
        value = value if shift == 0 else shifted(value, shift)
        for half in range(2):
            wst_v[i, half] = value[half]
    for half in range(2):
        pot_v[half, 0:8] = jnp.zeros((8, OY), F32)
        pot_v[half, 8 + ROWS:16 + ROWS] = jnp.zeros((8, OY), F32)

    take_block(mx0, mx_right, mx_left, rsem, MATRIX)
    mx_rt, mx_lf = mx_right[...], mx_left[...]
    mx1 = [beside(mx_rt, mx_lf, j) for j in range(2)]
    take(g_r.at[pl.ds(0, 95)], rsem.at[GATHER])
    even, odd = g_r[0:ROWS], g_r[ROWS:2 * ROWS]

    def column_of(block, point):
        return jnp.sum(jnp.where(lane_x == point, block, 0.0), axis=1, keepdims=True)

    near = jnp.zeros((ROWS, OY), F32)
    side = jnp.zeros((ROWS, OY), F32)
    for j in range(2):
        here = jnp.where(lane_x < 64, column_of(even, 2 * t + j), column_of(odd, 2 * t + j))
        there = jnp.where(
            lane_x < 64, column_of(even, 2 * right + j), column_of(odd, 2 * left + j)
        )
        near = near + mx0[j] * here
        side = side + mx1[j] * there
    forcing = (ocean_step * near, ocean_step * side)

    for _ in range(SUBCYCLES):
        for half in range(2):
            potential[half] = (
                (1.0 - friction) * potential[half]
                + ((ocean_step * wave_speed) * height[half] + forcing[half])
            )
            pot_v[half, 8:8 + ROWS] = potential[half]
        sums = [[], [], []]
        for half in range(2):
            above = pot_v[half, 7:7 + ROWS]
            below = pot_v[half, 9:9 + ROWS]
            for j in range(3):
                sums[j].append(
                    wst_v[3 * j, half] * above
                    + wst_v[3 * j + 1, half] * potential[half]
                    + wst_v[3 * j + 2, half] * below
                )
        west, east_sum = shifted(sums[0], 1), shifted(sums[2], -1)
        for half in range(2):
            height[half] = (height[half] + sums[1][half]) + (west[half] + east_sum[half])

    h_s[...] = height[0][own]
    u_r[pl.ds(own_q, 1)] = h_s[pl.ds(r, 1)]
    for to, chip in zip(peers, peer_chips):
        send(h_s.at[pl.ds(chip, 1)], u_r.at[pl.ds(own_q, 1)], UP, (c, to))
    result[PTS:PTS + OX] = height[0][own]
    result[PTS + OX:PTS + 2 * OX] = potential[0][own]

    atmos = finish(1, atmos, rate1)
    result[0:PTS] = atmos

    for i in (11, 12):
        loads[i].wait()
    take(tab_r.at[1, pl.ds(0, NR - 1)], rsem.at[TABLE_UP])
    upward = matrices(
        tab_r[1], (by_core(utgt_v) - 2 * peer_q).astype(F32), by_core(uwgt_v)
    )
    up_cells = []
    blank = jnp.zeros((NR, 128), F32)
    for j in range(2):
        low = jnp.where(k == 0, upward[j], blank)
        high = jnp.where(k == 0, blank, upward[j])
        up_cells.append(jnp.concatenate([low, high], axis=0).T[0:NR])

    take(edge_r.at[0, pl.ds(0, 24)], ssem.at[HALO])
    take(tab_r.at[0, pl.ds(0, NR - 1)], ssem.at[TABLE])
    take(tab_r.at[1, pl.ds(0, NR - 1)], ssem.at[TABLE_UP])
    take(edge_r.at[0, pl.ds(0, 52)], ssem.at[EDGE])
    take(edge_r.at[1, pl.ds(0, 52)], ssem.at[EDGE + 1])
    take_block(oc0, oc_right, oc_left, ssem, OCEAN)
    take_block(mx0, mx_right, mx_left, ssem, MATRIX)
    take(g_r.at[pl.ds(0, NR - 1)], ssem.at[GATHER])

    @pl.when(far == 1)
    def _():
        take(g_r.at[pl.ds(0, NR)], ssem.at[FAR])

    q_row = iota((AX, NR), 1)
    pick = jnp.where((q_row % 32) // 4 == iota((AX, NR), 0), 1.0, 0.0).astype(F32)
    column0 = 4 * (row_q % 4) + 2 * (row_q // 32)
    take(u_r.at[pl.ds(0, NR - 1)], rsem.at[UP])
    cells = u_r[...]
    spread = jnp.zeros((NR, 128), F32)
    for j in range(2):
        total = jnp.sum(up_cells[j] * cells, axis=1, keepdims=True)
        spread = spread + jnp.where(lane_64 == column0 + j, total, 0.0)
    flux = lax.dot_general(pick, spread, NN, precision=HIGHEST, preferred_element_type=F32)
    result[PTS + 2 * OX:PTS + 2 * OX + AX] = flux
    take(u_r.at[pl.ds(0, NR - 1)], ssem.at[UP])


def hand_out(result, atmos_out, height_out, potential_out, flux_out, flux_v, sem):
    flux_v[...] = result[PTS + 2 * OX:PTS + 2 * OX + AX, 0:AY]
    copies = [
        pltpu.make_async_copy(src, dst, sem.at[i])
        for i, (src, dst) in enumerate([
            (result.at[pl.ds(0, PTS)], atmos_out),
            (result.at[pl.ds(PTS, OX)], height_out),
            (result.at[pl.ds(PTS + OX, OX)], potential_out),
            (flux_v, flux_out),
        ])
    ]
    for copy in copies:
        copy.start()
    for copy in copies:
        copy.wait()


def on_device(
    atmos_state, wind_field, ocean_height, ocean_potential, ocean_neighbors, ocean_coupling,
    downward_source, downward_target, downward_weight,
    upward_source, upward_target, upward_weight,
):
    table = lambda value: value.reshape(NR, 128)
    any_spec = pl.BlockSpec(memory_space=pl.ANY)
    vm = lambda *shape, dtype=F32: pltpu.VMEM(shape, dtype)
    i32 = jnp.int32
    total_rows = PTS + 2 * OX + AX
    packed = pl.pallas_call(
        kernel,
        out_shape=pltpu.VMEM((total_rows, 128), F32),
        in_specs=[any_spec] * 13,
        out_specs=pl.BlockSpec(memory_space=pltpu.VMEM),
        scratch_shapes=[
            vm(PTS, 128), vm(2 * PTS, 128, dtype=jnp.bfloat16),
            vm(6, OX, OY, dtype=i32), vm(6, OX, OY),
            vm(NR, 128, dtype=i32), vm(NR, 128, dtype=i32), vm(NR, 128),
            vm(NR, 128, dtype=i32), vm(NR, 128, dtype=i32), vm(NR, 128),
            vm(6 * PTS, PTS, dtype=jnp.bfloat16),
            vm(3, 16, PTS), vm(2, NR, 128), vm(2, NR, 128), vm(2, 48, 128), vm(2, 56, 128),
            vm(8, ROWS, OY), vm(OX, OY), vm(ROWS, OY), vm(ROWS, OY),
            vm(2, ROWS, OY), vm(OX, OY), vm(ROWS, OY), vm(ROWS, OY),
            vm(8, 128), vm(2 * ROWS, 128), vm(OX, OY), vm(NR, 128),
            vm(2, NR, 128), vm(9, 2, ROWS, OY), vm(2, ROWS + 16, OY),
            pltpu.SemaphoreType.DMA((13,)),
            pltpu.SemaphoreType.DMA((14,)), pltpu.SemaphoreType.DMA((13,)),
        ],
        compiler_params=pltpu.CompilerParams(
            collective_id=0, has_side_effects=True, vmem_limit_bytes=60 * 1024 * 1024
        ),
        name="coupled_step",
    )(
        atmos_state.reshape(PTS, 128), wind_field.reshape(2 * PTS, 128),
        ocean_height, ocean_potential, ocean_neighbors, ocean_coupling,
        table(downward_source), table(downward_target), table(downward_weight),
        table(upward_source), table(upward_target), table(upward_weight),
        jnp.asarray(split_operators()),
    )
    outs = pl.pallas_call(
        hand_out,
        out_shape=[
            jax.ShapeDtypeStruct((PTS, 128), F32),
            jax.ShapeDtypeStruct((OX, OY), F32),
            jax.ShapeDtypeStruct((OX, OY), F32),
            jax.ShapeDtypeStruct((AX, AY), F32),
        ],
        in_specs=[pl.BlockSpec(memory_space=pltpu.VMEM)],
        out_specs=[any_spec] * 4,
        scratch_shapes=[vm(AX, AY), pltpu.SemaphoreType.DMA((4,))],
        name="hand_out",
    )(pltpu.with_memory_space_constraint(packed, pltpu.VMEM))
    return (outs[0].reshape(AX, AY, 128), outs[1], outs[2], outs[3])


def solution(mesh):
    cells = P(None, "comp", "tile")
    tables = P("comp", "tile", None)
    flat = P("comp", "tile")
    return jax.shard_map(
        on_device,
        mesh=mesh,
        in_specs=(tables, P(None, "comp", "tile", None), flat, flat, cells, cells) + (tables,) * 6,
        out_specs=(tables, flat, flat, flat),
        check_vma=False,
    )
```
